32 devices in a mesh: seq: 4 (over y, x), dp: 8 (over z, core).
Axes of the slice: x: 2, y: 2, z: 4, core: 2. Of those that a mesh axis runs over, the one named last changes fastest.
Arguments:
- tokens: bfloat16 [8, 4, 784, 512], P('dp', 'seq'), may hold values from -6 to 6
- cotangent: bfloat16 [8, 4, 784, 512], P('dp', 'seq'), may hold values from -6 to 6
- norm1_gain: bfloat16 [512], P('dp'), may hold values from 0.25 to 1.75
- norm1_bias: bfloat16 [512], P('dp'), may hold values from -1.75 to 1.75
- qkv_weight: bfloat16 [512, 1536], P('dp'), may hold values from -0.25 to 0.25
- query_bias: bfloat16 [512], P('dp'), may hold values from -1.75 to 1.75
- value_bias: bfloat16 [512], P('dp'), may hold values from -1.75 to 1.75
- proj_weight: bfloat16 [512, 512], P('dp'), may hold values from -1 to 1
- proj_bias: bfloat16 [512], P('dp'), may hold values from -1.75 to 1.75
- norm2_gain: bfloat16 [512], P('dp'), may hold values from 0.25 to 1.75
- norm2_bias: bfloat16 [512], P('dp'), may hold values from -1.75 to 1.75
- fc1_weight: bfloat16 [512, 2048], P('dp'), may hold values from -0.25 to 0.25
- fc1_bias: bfloat16 [2048], P('dp'), may hold values from -1.75 to 1.75
- fc2_weight: bfloat16 [2048, 512], P('dp'), may hold values from -0.125 to 0.125
- fc2_bias: bfloat16 [512], P('dp'), may hold values from -1.75 to 1.75
- bias_table: float32 [169, 16], replicated, may hold values from -6 to 6
- region_ids: int32 [56, 56], replicated, may hold values from 0 to 8, as said below
- rel_index: int32 [49, 49], replicated, may hold values from 0 to 168, as said below
Outputs:
- output: bfloat16 [8, 4, 784, 512], P('dp', 'seq')
- input_grad: bfloat16 [8, 4, 784, 512], P('dp', 'seq')
- grad_norm1_gain: float32 [512], P('dp')
- grad_norm1_bias: float32 [512], P('dp')
- grad_qkv_weight: float32 [512, 1536], P('dp')
- grad_query_bias: float32 [512], P('dp')
- grad_value_bias: float32 [512], P('dp')
- grad_proj_weight: float32 [512, 512], P('dp')
- grad_proj_bias: float32 [512], P('dp')
- grad_norm2_gain: float32 [512], P('dp')
- grad_norm2_bias: float32 [512], P('dp')
- grad_fc1_weight: float32 [512, 2048], P('dp')
- grad_fc1_bias: float32 [2048], P('dp')
- grad_fc2_weight: float32 [2048, 512], P('dp')
- grad_fc2_bias: float32 [512], P('dp')
- grad_bias_table: float32 [169, 16], replicated
The draws below stay inside these ranges and needn't reach their ends.
Inputs may be any that keep to these rules, and one draw needn't show every extreme that they name: region_ids[i, j] = 3 a_i + b_j, where each row i has its own a_i and each column j its own b_j, both 0, 1 or 2; all nine values occur. rel_index[a, b] depends only on the offset between positions a and b of the 7 x 7 window (row-major); different offsets give different rows, and every row of the table is used.
All inputs are finite; a program needn't handle non-finite values.
Results may differ from the reference program's by a relative error of at most 0.019.
Values may be sent and summed in bfloat16 or wider, within the bound.
A program may use at most 128 MiB of HBM per device.

```python
import jax
import jax.numpy as jnp
from jax import lax

D = 512
HEADS = 16
MLP = 2048
TABLE = 169
IMG_H = 56
IMG_W = 56
IMAGES = 8
TILE_TOK = 784
N_SEQ = 4


def band_numbers(key_pick, key_start, count):
    picks = jax.random.randint(key_pick, (count,), 0, 3).astype(jnp.int32)
    start = jax.random.randint(key_start, (), 0, 3).astype(jnp.int32)
    places = jnp.arange(count, dtype=jnp.int32)
    leading = ((places + start) % 3).astype(jnp.int32)
    return jnp.where(places < 3, leading, picks).astype(jnp.int32)


def draw_region_ids(key, part):
    key = jax.random.fold_in(key, 5)
    keys = jax.random.split(key, 4)
    band_rows = band_numbers(keys[0], keys[1], IMG_H)
    band_cols = band_numbers(keys[2], keys[3], IMG_W)
    return (3 * band_rows[:, None] + band_cols[None, :]).astype(jnp.int32)


def draw_rel_index(key, part):
    key = jax.random.fold_in(key, 9)
    order = jax.random.permutation(key, TABLE).astype(jnp.int32)
    spots = jnp.arange(49, dtype=jnp.int32)
    rows = spots // 7
    cols = spots % 7
    base = (rows[:, None] - rows[None, :] + 6) * 13 + (cols[:, None] - cols[None, :] + 6)
    return order[base].astype(jnp.int32)


def levels(own_key, extent, pieces, smallest, largest):
    level = 1.0
    for axis_at, shards_of in pieces:
        draws = jax.random.uniform(jax.random.fold_in(jax.random.fold_in(own_key, 6), axis_at), (shards_of,), jnp.float32, smallest / len(pieces), largest / len(pieces))
        level = level * jnp.repeat(jnp.exp(draws), extent[axis_at] // shards_of).reshape((-1,) + (1,) * (len(extent) - 1 - axis_at))
    return level


def scatter_about(rng, dims, scale, reach, pieces=(), kind=jnp.bfloat16):
    factor_of = levels(rng, dims, pieces, -0.22, 0.18) if pieces else 1.0
    drawn = jax.random.normal(rng, dims, jnp.float32) * scale * factor_of
    return jnp.minimum(jnp.maximum(drawn, -reach), reach).astype(kind)


def setup_inputs(seed: int = 0) -> dict:
    arg_keys = jax.random.split(jax.random.key(seed), 19)
    tokens = scatter_about(arg_keys[0], (IMAGES, N_SEQ, TILE_TOK, D), 1.0, 6.0, ((0, 8), (1, 4)))
    cotangent = scatter_about(arg_keys[1], (IMAGES, N_SEQ, TILE_TOK, D), 1.0, 6.0, ((0, 8), (1, 4)))
    norm1_gain = jnp.clip(1.0 + 0.15 * jax.random.normal(arg_keys[2], (D,), jnp.float32), 0.25, 1.75).astype(jnp.bfloat16)
    norm1_bias = scatter_about(arg_keys[3], (D,), 0.3, 1.75, ((0, 8),))
    qkv_weight = scatter_about(arg_keys[4], (D, 3 * D), D ** -0.5, 0.25, ((0, 8),))
    query_bias = scatter_about(arg_keys[5], (D,), 0.3, 1.75, ((0, 8),))
    value_bias = scatter_about(arg_keys[6], (D,), 0.3, 1.75, ((0, 8),))
    proj_weight = scatter_about(arg_keys[7], (D, D), (D // 16) ** -0.5, 1.0, ((0, 8),))
    proj_bias = scatter_about(arg_keys[8], (D,), 0.3, 1.75, ((0, 8),))
    norm2_gain = jnp.clip(1.0 + 0.15 * jax.random.normal(arg_keys[9], (D,), jnp.float32), 0.25, 1.75).astype(jnp.bfloat16)
    norm2_bias = scatter_about(arg_keys[10], (D,), 0.3, 1.75, ((0, 8),))
    fc1_weight = scatter_about(arg_keys[11], (D, MLP), D ** -0.5, 0.25, ((0, 8),))
    fc1_bias = scatter_about(arg_keys[12], (MLP,), 0.3, 1.75, ((0, 8),))
    fc2_weight = scatter_about(arg_keys[13], (MLP, D), MLP ** -0.5, 0.125, ((0, 8),))
    fc2_bias = scatter_about(arg_keys[14], (D,), 0.3, 1.75, ((0, 8),))
    bias_table = scatter_about(arg_keys[15], (TABLE, HEADS), 1.0, 6.0, (), jnp.float32)
    region_ids = draw_region_ids(jax.random.fold_in(arg_keys[18], 71), 0)
    rel_index = draw_rel_index(jax.random.fold_in(arg_keys[18], 71), 0)
    return dict(tokens=tokens, cotangent=cotangent, norm1_gain=norm1_gain, norm1_bias=norm1_bias, qkv_weight=qkv_weight, query_bias=query_bias, value_bias=value_bias, proj_weight=proj_weight, proj_bias=proj_bias, norm2_gain=norm2_gain, norm2_bias=norm2_bias, fc1_weight=fc1_weight, fc1_bias=fc1_bias, fc2_weight=fc2_weight, fc2_bias=fc2_bias, bias_table=bias_table, region_ids=region_ids, rel_index=rel_index)


@jax.custom_vjp
def low(v):
    return lax.optimization_barrier(v.astype(jnp.bfloat16)).astype(jnp.float32)

@jax.custom_vjp
def low_back(v):
    return v

def low_keep(v):
    return (low(v), None)

def low_pass(kept, grad):
    return (grad,)

def back_keep(v):
    return (v, None)

def back_low(kept, grad):
    return (low(grad),)
low.defvjp(low_keep, low_pass)
low_back.defvjp(back_keep, back_low)
HIGHEST = lax.Precision.HIGHEST

def matmul(left, right):
    return jnp.dot(left, right, precision=HIGHEST)

def layer_norm(values, gain, shift):
    centered = values - lax.optimization_barrier(jnp.mean(values, -1, keepdims=True))
    spread = lax.optimization_barrier(jnp.mean(centered * centered, -1, keepdims=True))
    return centered * lax.rsqrt(spread + 1e-05) * gain + shift

def to_image(tiles):
    width = tiles.shape[-1]
    grid = tiles.reshape(N_SEQ // 2, 2, IMG_H // 2, IMG_W * 2 // N_SEQ, width)
    return grid.transpose(1, 2, 0, 3, 4).reshape(IMG_H, IMG_W, width)

def to_tiles(image):
    width = image.shape[-1]
    grid = image.reshape(2, IMG_H // 2, N_SEQ // 2, IMG_W * 2 // N_SEQ, width)
    return grid.transpose(2, 0, 1, 3, 4).reshape(N_SEQ, IMG_H // 2 * (IMG_W * 2 // N_SEQ), width)

def windows(image):
    rows, cols, width = image.shape
    return image.reshape(rows // 7, 7, cols // 7, 7, width).transpose(0, 2, 1, 3, 4).reshape(-1, 49, width)

def unwindows(blocks, rows, cols):
    width = blocks.shape[-1]
    return blocks.reshape(rows // 7, cols // 7, 7, 7, width).transpose(0, 2, 1, 3, 4).reshape(rows, cols, width)

def layer(image, params, table, mask, onehot):
    gain_one, shift_one, qkv_weight, query_bias, value_bias, proj_weight, proj_bias, gain_two, shift_two, fc1_weight, fc1_bias, fc2_weight, fc2_bias = params
    dim = image.shape[-1]
    heads = table.shape[1]
    size = dim // heads
    normed = low(low_back(layer_norm(image, gain_one, shift_one)))
    shifted = jnp.roll(normed, (-3, -3), (0, 1))
    flat = windows(shifted).reshape(-1, dim)
    projected = matmul(flat, qkv_weight) + jnp.concatenate([query_bias, jnp.zeros_like(query_bias), value_bias])
    queries = low(low_back(projected[:, :dim])).reshape(-1, 49, heads, size)
    keys = low(low_back(projected[:, dim:2 * dim])).reshape(-1, 49, heads, size)
    values = low(low_back(projected[:, 2 * dim:])).reshape(-1, 49, heads, size)
    bias = matmul(onehot, table).reshape(49, 49, heads).transpose(2, 0, 1)
    scores = jnp.einsum('wqhe,wkhe->whqk', queries, keys, precision=HIGHEST) * size ** (-0.5) + bias[None] + mask[:, None]
    scores = low_back(scores)
    probs = low(jax.nn.softmax(scores, axis=-1))
    mixed = jnp.einsum('whqk,wkhe->wqhe', probs, values, precision=HIGHEST)
    mixed = low(low_back(mixed)).reshape(-1, 49, dim)
    restored = jnp.roll(unwindows(mixed, IMG_H, IMG_W), (3, 3), (0, 1)).reshape(-1, dim)
    resid = image.reshape(-1, dim) + low_back(matmul(restored, proj_weight)) + proj_bias
    second = low(layer_norm(resid, gain_two, shift_two))
    before = low_back(matmul(second, fc1_weight) + fc1_bias)
    hidden = low(jax.nn.gelu(before, approximate=False))
    result = resid + matmul(hidden, fc2_weight) + fc2_bias
    return result.reshape(image.shape)

def reference(tokens, cotangent, norm1_gain, norm1_bias, qkv_weight, query_bias, value_bias, proj_weight, proj_bias, norm2_gain, norm2_bias, fc1_weight, fc1_bias, fc2_weight, fc2_bias, bias_table, region_ids, rel_index):
    params = tuple((p.astype(jnp.float32) for p in (norm1_gain, norm1_bias, qkv_weight, query_bias, value_bias, proj_weight, proj_bias, norm2_gain, norm2_bias, fc1_weight, fc1_bias, fc2_weight, fc2_bias)))
    table = bias_table.astype(jnp.float32)
    region_win = windows(region_ids[:, :, None])[:, :, 0]
    mask = jnp.where(region_win[:, :, None] == region_win[:, None, :], 0.0, -100.0).astype(jnp.float32)
    onehot = (rel_index.reshape(-1)[:, None] == jnp.arange(table.shape[0], dtype=jnp.int32)[None, :]).astype(jnp.float32)

    def one(total, item):
        tiles, grad_tiles = item
        image = to_image(tiles.astype(jnp.float32))

        def apply(image, params, table):
            return layer(image, params, table, mask, onehot)
        result, pull = jax.vjp(apply, image, params, table)
        grad_image, grad_params, grad_table = pull(to_image(grad_tiles.astype(jnp.float32)))
        total = jax.tree.map(jnp.add, total, (grad_params, grad_table))
        return (total, (to_tiles(result).astype(jnp.bfloat16), to_tiles(grad_image).astype(jnp.bfloat16)))
    start = jax.tree.map(jnp.zeros_like, (params, table))
    (grad_params, grad_table), (outputs, grads) = lax.scan(one, start, (tokens, cotangent))
    return (outputs, grads, grad_params[0], grad_params[1], grad_params[2], grad_params[3], grad_params[4], grad_params[5], grad_params[6], grad_params[7], grad_params[8], grad_params[9], grad_params[10], grad_params[11], grad_params[12], grad_table)
```

```python
import functools

import jax
import jax.numpy as jnp
from jax import lax
from jax.experimental import pallas as pl
from jax.experimental.pallas import tpu as pltpu
from jax.sharding import PartitionSpec as P

HIGHEST = lax.Precision.HIGHEST
F32 = jnp.float32
BF16 = jnp.bfloat16
SIDE = 7
CELLS = SIDE * SIDE
ROWS = 56
PAIR = 2 * ROWS
VMEM = 56 * 1024 * 1024


def send(value, rows, cols):
    count = lax.axis_size("seq")
    wide = count // 2
    pairs = []
    for place in range(count):
        r, c = place % 2, place // 2
        source = (c + cols) % wide * 2 + (r + rows) % 2
        pairs.append((source, place))
    return lax.ppermute(value, "seq", pairs)


def roll_ahead(field):
    below = send(field[:, :3, 3:], 1, 0)
    beside = send(field[:, 3:, :3], 0, 1)
    corner = send(field[:, :3, :3], 1, 1)
    top = jnp.concatenate([field[:, 3:, 3:], beside], 2)
    low = jnp.concatenate([below, corner], 2)
    return jnp.concatenate([top, low], 1)


def roll_behind(field):
    above = send(field[:, -3:, :-3], -1, 0)
    beside = send(field[:, :-3, -3:], 0, -1)
    corner = send(field[:, -3:, -3:], -1, -1)
    top = jnp.concatenate([corner, above], 2)
    low = jnp.concatenate([beside, field[:, :-3, :-3]], 2)
    return jnp.concatenate([top, low], 1)


def to_windows(field):
    batch, rows, cols, width = field.shape
    return (
        field.reshape(batch, rows // SIDE, SIDE, cols // SIDE, SIDE, width)
        .transpose(0, 1, 3, 2, 4, 5)
        .reshape(-1, CELLS, width)
    )


def from_windows(blocks, batch, rows, cols):
    width = blocks.shape[-1]
    return (
        blocks.reshape(batch, rows // SIDE, cols // SIDE, SIDE, SIDE, width)
        .transpose(0, 1, 3, 2, 4, 5)
        .reshape(batch, rows, cols, width)
    )


def pad_windows(field):
    return jnp.pad(to_windows(field), ((0, 0), (0, ROWS - CELLS), (0, 0))).reshape(
        -1, field.shape[-1]
    )


def stack_heads(block, per):
    part = lax.broadcasted_iota(jnp.int32, block.shape, 1) // (block.shape[1] // per)
    return jnp.concatenate([jnp.where(part == j, block, jnp.zeros_like(block)) for j in range(per)], 0)


def merge_heads(tall, per):
    rows = tall.shape[0] // per
    part = lax.broadcasted_iota(jnp.int32, (rows, tall.shape[1]), 1) // (tall.shape[1] // per)
    total = jnp.where(part == 0, tall[:rows], 0.0)
    for j in range(1, per):
        total = jnp.where(part == j, tall[j * rows : (j + 1) * rows], total)
    return total


def dot_nt(left, right):
    return lax.dot_general(left, right, (((1,), (1,)), ((), ())), preferred_element_type=F32)


def dot_tn(left, right):
    return lax.dot_general(left, right, (((0,), (0,)), ((), ())), preferred_element_type=F32)


def dot_nn(left, right):
    return jnp.dot(left, right, preferred_element_type=F32)


def attend_kernel(scale, per, qkv_ref, bias_ref, mask_ref, o_ref, p_ref):
    dim = o_ref.shape[1]
    tall = per * PAIR
    mask = mask_ref[0]
    for g in range(dim // 128):
        at = slice(g * 128, (g + 1) * 128)
        band = slice(g * tall, (g + 1) * tall)
        q = stack_heads(qkv_ref[:, g * 128 : (g + 1) * 128], per)
        k = qkv_ref[:, dim + g * 128 : dim + (g + 1) * 128]
        v = qkv_ref[:, 2 * dim + g * 128 : 2 * dim + (g + 1) * 128]
        s = dot_nt(q, k) * scale + bias_ref[band, :]
        s = (s.reshape(per, PAIR, PAIR) + mask[None]).reshape(tall, PAIR)
        e = jnp.exp(s - jnp.max(s, -1, keepdims=True))
        p = (e * (1.0 / jnp.sum(e, -1, keepdims=True))).astype(BF16)
        p_ref[0, band, :] = p
        o_ref[:, at] = merge_heads(dot_nn(p, v), per).astype(BF16)


def attend_back_kernel(scale, per, qkv_ref, do_ref, p_ref, dqkv_ref, sum_ref):
    dim = do_ref.shape[1]
    tall = per * PAIR

    @pl.when(pl.program_id(0) == 0)
    def _():
        sum_ref[...] = jnp.zeros_like(sum_ref)

    for g in range(dim // 128):
        band = slice(g * tall, (g + 1) * tall)
        q = stack_heads(qkv_ref[:, g * 128 : (g + 1) * 128], per)
        k = qkv_ref[:, dim + g * 128 : dim + (g + 1) * 128]
        v = qkv_ref[:, 2 * dim + g * 128 : 2 * dim + (g + 1) * 128]
        do = stack_heads(do_ref[:, g * 128 : (g + 1) * 128], per)
        p = p_ref[0, band, :]
        pf = p.astype(F32)
        dp = dot_nt(do, v)
        dl = (pf * (dp - jnp.sum(dp * pf, -1, keepdims=True))).astype(BF16)
        sum_ref[band, :] += dl.astype(F32)
        dq = merge_heads(dot_nn(dl, k), per) * scale
        dk = dot_tn(dl, q) * scale
        dv = dot_tn(p, do)
        dqkv_ref[:, g * 128 : (g + 1) * 128] = dq.astype(BF16)
        dqkv_ref[:, dim + g * 128 : dim + (g + 1) * 128] = dk.astype(BF16)
        dqkv_ref[:, 2 * dim + g * 128 : 2 * dim + (g + 1) * 128] = dv.astype(BF16)


def attend(qkv, bias, mask, heads):
    rows, dim = qkv.shape[0], qkv.shape[1] // 3
    pairs = rows // PAIR
    per = 128 * heads // dim
    return pl.pallas_call(
        functools.partial(attend_kernel, (dim // heads) ** -0.5, per),
        grid=(pairs,),
        out_shape=(
            jax.ShapeDtypeStruct((rows, dim), BF16),
            jax.ShapeDtypeStruct((pairs, heads * PAIR, PAIR), BF16),
        ),
        in_specs=[
            pl.BlockSpec((PAIR, 3 * dim), lambda i: (i, 0)),
            pl.BlockSpec((heads * PAIR, PAIR), lambda i: (0, 0)),
            pl.BlockSpec((1, PAIR, PAIR), lambda i: (i, 0, 0)),
        ],
        out_specs=(
            pl.BlockSpec((PAIR, dim), lambda i: (i, 0)),
            pl.BlockSpec((1, heads * PAIR, PAIR), lambda i: (i, 0, 0)),
        ),
        compiler_params=pltpu.CompilerParams(vmem_limit_bytes=VMEM),
        cost_estimate=pl.CostEstimate(
            flops=4 * rows * heads * PAIR * 128, bytes_accessed=rows * dim * 8, transcendentals=rows * heads * 128
        ),
    )(qkv, bias, mask)


def attend_back(qkv, grad, probs, heads):
    rows, dim = grad.shape
    pairs = rows // PAIR
    per = 128 * heads // dim
    return pl.pallas_call(
        functools.partial(attend_back_kernel, (dim // heads) ** -0.5, per),
        grid=(pairs,),
        out_shape=(
            jax.ShapeDtypeStruct((rows, 3 * dim), BF16),
            jax.ShapeDtypeStruct((heads * PAIR, PAIR), F32),
        ),
        in_specs=[
            pl.BlockSpec((PAIR, 3 * dim), lambda i: (i, 0)),
            pl.BlockSpec((PAIR, dim), lambda i: (i, 0)),
            pl.BlockSpec((1, heads * PAIR, PAIR), lambda i: (i, 0, 0)),
        ],
        out_specs=(
            pl.BlockSpec((PAIR, 3 * dim), lambda i: (i, 0)),
            pl.BlockSpec((heads * PAIR, PAIR), lambda i: (0, 0)),
        ),
        compiler_params=pltpu.CompilerParams(vmem_limit_bytes=VMEM),
        cost_estimate=pl.CostEstimate(
            flops=8 * rows * heads * PAIR * 128, bytes_accessed=rows * dim * 16, transcendentals=0
        ),
    )(qkv, grad, probs)


def normalize(values):
    center = values - jnp.mean(values, -1, keepdims=True)
    scaled = lax.rsqrt(jnp.mean(center * center, -1, keepdims=True) + 1e-05)
    return center * scaled, scaled


def normalize_back(grad, unit, scaled, gain):
    inner = grad * gain
    return scaled * (
        inner
        - jnp.mean(inner, -1, keepdims=True)
        - unit * jnp.mean(inner * unit, -1, keepdims=True)
    )


def gather_rows(weight):
    share = weight.shape[0] // lax.axis_size("seq")
    mine = lax.dynamic_slice_in_dim(weight, lax.axis_index("seq") * share, share, 0)
    return lax.all_gather(mine, ("dp", "seq"), axis=0, tiled=True)


def reduce_rows(grad):
    part = lax.psum_scatter(grad.astype(BF16), ("dp", "seq"), scatter_dimension=0, tiled=True)
    return lax.all_gather(part, "seq", axis=0, tiled=True).astype(F32)


def local(
    tokens,
    cotangent,
    norm1_gain,
    norm1_bias,
    qkv_weight,
    query_bias,
    value_bias,
    proj_weight,
    proj_bias,
    norm2_gain,
    norm2_bias,
    fc1_weight,
    fc1_bias,
    fc2_weight,
    fc2_bias,
    bias_table,
    region_ids,
    rel_index,
):
    batch = tokens.shape[0]
    dim = tokens.shape[-1]
    heads = bias_table.shape[1]
    image_rows, image_cols = region_ids.shape
    seq_count = lax.axis_size("seq")
    tile_rows = image_rows // 2
    tile_cols = image_cols * 2 // seq_count
    place = lax.axis_index("seq")

    smalls = [
        norm1_gain, norm1_bias, query_bias, value_bias, proj_bias, norm2_gain, norm2_bias, fc2_bias, fc1_bias,
    ]
    small_all = lax.all_gather(jnp.concatenate(smalls), "dp", axis=0, tiled=False)
    full, at = [], 0
    for s in smalls:
        full.append(small_all[:, at : at + s.shape[0]].reshape(-1).astype(F32))
        at += s.shape[0]
    gain_one, shift_one, qbias, vbias, pbias, gain_two, shift_two, fc2b, fc1b = full
    qkv_full = gather_rows(qkv_weight)
    proj_full = gather_rows(proj_weight)
    fc1_full = gather_rows(fc1_weight)
    fc2_full = gather_rows(fc2_weight)

    regions = lax.dynamic_slice(
        region_ids, (place % 2 * tile_rows, place // 2 * tile_cols), (tile_rows, tile_cols)
    )
    region_win = to_windows(regions[None, :, :, None])[:, :, 0]
    mask = jnp.where(region_win[:, :, None] == region_win[:, None, :], 0.0, -100.0).astype(F32)
    mask = jnp.tile(mask, (batch, 1, 1))
    low = -1e30
    mask = jnp.pad(mask, ((0, 0), (0, 0), (0, ROWS - CELLS)), constant_values=low)
    mask = jnp.pad(mask, ((0, 0), (0, ROWS - CELLS), (0, 0)))
    mask = mask.at[:, CELLS:, CELLS:].set(low)
    mask = mask.reshape(-1, 2, ROWS, ROWS)
    other = jnp.full_like(mask[:, 0], low)
    mask = jnp.concatenate(
        [jnp.concatenate([mask[:, 0], other], 2), jnp.concatenate([other, mask[:, 1]], 2)], 1
    )
    onehot = (
        rel_index.reshape(-1)[:, None] == jnp.arange(bias_table.shape[0], dtype=jnp.int32)[None, :]
    ).astype(F32)
    bias = jnp.dot(onehot, bias_table, precision=HIGHEST).reshape(CELLS, CELLS, heads).transpose(2, 0, 1)
    bias = jnp.pad(bias, ((0, 0), (0, ROWS - CELLS), (0, ROWS - CELLS)))
    bias = jnp.tile(bias, (1, 2, 2)).reshape(heads * PAIR, PAIR)

    source = pad_windows(roll_ahead(tokens.reshape(batch, tile_rows, tile_cols, dim)))
    grad_out = pad_windows(roll_ahead(cotangent.reshape(batch, tile_rows, tile_cols, dim)))
    source = source.astype(F32)

    unit_one, scaled_one = normalize(source)
    first = (unit_one * gain_one + shift_one).astype(BF16)
    qkv_bias = jnp.concatenate([qbias, jnp.zeros((dim,), F32), vbias])
    qkv = (dot_nn(first, qkv_full) + qkv_bias).astype(BF16)
    mixed, probs = attend(qkv, bias, mask, heads)
    resid = source + dot_nn(mixed, proj_full) + pbias
    unit_two, scaled_two = normalize(resid)
    second = (unit_two * gain_two + shift_two).astype(BF16)
    before = dot_nn(second, fc1_full) + fc1b
    normal_cdf = 0.5 * (1.0 + lax.erf(before * 0.7071067811865476))
    hidden = (before * normal_cdf).astype(BF16)
    output = (resid + dot_nn(hidden, fc2_full) + fc2b).astype(BF16)

    def to_tile(field):
        field = field.reshape(-1, ROWS, dim)[:, :CELLS]
        return roll_behind(from_windows(field, batch, tile_rows, tile_cols)).reshape(tokens.shape)

    output = to_tile(output)

    grad_fc2 = dot_tn(hidden, grad_out)
    grad_fc2b = jnp.sum(grad_out.astype(F32), 0)
    grad_hidden = dot_nt(grad_out, fc2_full)
    normal_pdf = jnp.exp(-0.5 * before * before) * 0.3989422804014327
    grad_before = (grad_hidden * (normal_cdf + before * normal_pdf)).astype(BF16)
    grad_fc1 = dot_tn(second, grad_before)
    grad_fc1b = jnp.sum(grad_before.astype(F32), 0)
    grad_second = dot_nt(grad_before, fc1_full)
    grad_gain2 = jnp.sum(grad_second * unit_two, 0)
    grad_shift2 = jnp.sum(grad_second, 0)
    grad_resid = grad_out.astype(F32) + normalize_back(grad_second, unit_two, scaled_two, gain_two)
    grad_pbias = jnp.sum(grad_resid, 0)
    grad_branch = grad_resid.astype(BF16)
    grad_proj = dot_tn(mixed, grad_branch)
    grad_mixed = dot_nt(grad_branch, proj_full).astype(BF16)
    grad_qkv_rows, score_sum = attend_back(qkv, grad_mixed, probs, heads)
    score_sum = score_sum.reshape(heads, PAIR, PAIR)
    score_sum = score_sum[:, :CELLS, :CELLS] + score_sum[:, ROWS : ROWS + CELLS, ROWS : ROWS + CELLS]
    grad_table = jnp.dot(
        onehot.T, score_sum.transpose(1, 2, 0).reshape(-1, heads), precision=HIGHEST
    )
    grad_qkv = dot_tn(first, grad_qkv_rows)
    grad_qkvb = jnp.sum(grad_qkv_rows.astype(F32), 0)
    grad_first = dot_nt(grad_qkv_rows, qkv_full).astype(BF16).astype(F32)
    grad_gain1 = jnp.sum(grad_first * unit_one, 0)
    grad_shift1 = jnp.sum(grad_first, 0)
    input_grad = normalize_back(grad_first, unit_one, scaled_one, gain_one) + grad_resid
    input_grad = to_tile(input_grad.astype(BF16))

    sum_fc2 = reduce_rows(grad_fc2)
    sum_fc1 = reduce_rows(grad_fc1)
    sum_proj = reduce_rows(grad_proj)
    sum_qkv = reduce_rows(grad_qkv)
    count = lax.axis_size("dp")
    vectors = [
        grad_gain1, grad_shift1, grad_qkvb[:dim], grad_qkvb[2 * dim :], grad_pbias, grad_gain2,
        grad_shift2, grad_fc2b, grad_fc1b,
    ]
    joined = lax.psum(jnp.concatenate(vectors + [grad_table.reshape(-1)]), ("dp", "seq"))
    owned, at = [], 0
    for v in vectors:
        size = v.shape[0] // count
        owned.append(lax.dynamic_slice(joined, (at + lax.axis_index("dp") * size,), (size,)))
        at += v.shape[0]
    table_total = joined[at:].reshape(bias_table.shape)
    s_gain1, s_shift1, s_qb, s_vb, s_pb, s_gain2, s_shift2, s_fc2b, s_fc1b = owned
    return (
        output,
        input_grad,
        s_gain1,
        s_shift1,
        sum_qkv,
        s_qb,
        s_vb,
        sum_proj,
        s_pb,
        s_gain2,
        s_shift2,
        sum_fc1,
        s_fc1b,
        sum_fc2,
        s_fc2b,
        table_total,
    )


def solution(mesh):
    rows, vector, matrix, whole = P("dp", "seq", None, None), P("dp"), P("dp", None), P()
    params = (
        vector, vector, matrix, vector, vector, matrix, vector, vector, vector, matrix, vector, matrix, vector,
    )
    in_specs = (rows, rows) + params + (whole, whole, whole)
    out_specs = (rows, rows) + params + (whole,)
    return jax.shard_map(local, mesh=mesh, in_specs=in_specs, out_specs=out_specs, check_vma=False)
```

```python
import functools

import jax
import jax.numpy as jnp
from jax import lax
from jax.experimental import pallas as pl
from jax.experimental.pallas import tpu as pltpu
from jax.sharding import PartitionSpec as P

HIGHEST = lax.Precision.HIGHEST
F32 = jnp.float32
BF16 = jnp.bfloat16
SIDE = 7
CELLS = SIDE * SIDE
ROWS = 56
PAIR = 2 * ROWS
VMEM = 56 * 1024 * 1024


MESH = pl.DeviceIdType.MESH
TILE = 16
STEP = 3


def edges_ahead(field):
    return field[:, :STEP, STEP:], field[:, STEP:, :STEP], field[:, :STEP, :STEP]


def edges_behind(field):
    return field[:, -STEP:, :-STEP], field[:, :-STEP, -STEP:], field[:, -STEP:, -STEP:]


def join_ahead(field, below, beside, corner):
    top = jnp.concatenate([field[:, STEP:, STEP:], beside], 2)
    return jnp.concatenate([top, jnp.concatenate([below, corner], 2)], 1)


def join_behind(field, above, beside, corner):
    low = jnp.concatenate([beside, field[:, :-STEP, :-STEP]], 2)
    return jnp.concatenate([jnp.concatenate([corner, above], 2), low], 1)


def pack_edges(edges):
    packed = []
    for blocks in zip(*edges):
        rows = jnp.concatenate([b.reshape(-1, b.shape[-1]) for b in blocks], 0)
        packed.append(jnp.pad(rows, ((0, -rows.shape[0] % TILE), (0, 0))))
    return packed


def unpack_edges(packed, edges):
    fields = [[] for _ in edges]
    for rows, blocks in zip(packed, zip(*edges)):
        at = 0
        for field, b in zip(fields, blocks):
            size = b.size // b.shape[-1]
            field.append(rows[at : at + size].reshape(b.shape))
            at += size
    return fields


class Mail:
    def __init__(self, send, recv):
        self.send, self.recv, self.used, self.open = send, recv, 0, []

    def push(self, src, dst, seq, dp):
        copy = pltpu.make_async_remote_copy(
            src_ref=src,
            dst_ref=dst,
            send_sem=self.send.at[self.used],
            recv_sem=self.recv.at[self.used],
            device_id=(seq, dp),
            device_id_type=MESH,
        )
        copy.start()
        self.used += 1
        self.open.append(copy)
        return copy

    def close(self):
        for copy in self.open:
            copy.wait_send()


def places(n, nd):
    s, d = lax.axis_index("seq"), lax.axis_index("dp")
    core = d % 2
    row = s + 1 - 2 * (s % 2)
    col = (s + 2) % n
    one = (1 - core) * row + core * col
    two = core * row + (1 - core) * col
    return s, d, one, two, (s // 2 * 2 + 2) % n + 1 - s % 2


def greet(n, nd, s, d):
    barrier = pltpu.get_barrier_semaphore()
    for m in range(1, n):
        pl.semaphore_signal(barrier, inc=1, device_id=((s + m) % n, d), device_id_type=MESH)
    for m in range(1, nd):
        pl.semaphore_signal(barrier, inc=1, device_id=(s, (d + m) % nd), device_id_type=MESH)
    pl.semaphore_wait(barrier, n - 1 + nd - 1)


def edge_sends(mail, n, s, d, src, dst, cols):
    row = s + 1 - 2 * (s % 2)
    col = (s + 2 * cols + n) % n
    return [
        mail.push(src[0], dst[0], row, d),
        mail.push(src[1], dst[1], col, d),
        mail.push(src[2], dst[2], col + 1 - 2 * (col % 2), d),
    ]


def gather_kernel(n, nd, w_ref, e0, e1, e2, o_ref, f0, f1, f2, send, recv, own):
    s, d, one, two, far = places(n, nd)
    nz, core = nd // 2, d % 2
    z = d // 2
    mate = d + 1 - 2 * core
    quarter = w_ref.shape[0] // n

    def part(block, q):
        return o_ref.at[block, pl.ds(pl.multiple_of(q * quarter, TILE), quarter)]

    greet(n, nd, s, d)
    mail = Mail(send, recv)
    keep = pltpu.make_async_copy(w_ref, o_ref.at[d], own)
    keep.start()
    mine = w_ref.at[pl.ds(pl.multiple_of(s * quarter, TILE), quarter)]
    along = [mail.push(mine, part(d, s), s, (z + k) % nz * 2 + core) for k in range(1, nz)]
    waits = edge_sends(mail, n, s, d, (e0, e1, e2), (f0, f1, f2), -1)
    waits.append(mail.push(w_ref, o_ref.at[d], s, mate))
    blocks = [(z + nz - k) % nz * 2 + core for k in range(1, nz)]
    across = []
    for copy, block in zip(along, blocks):
        copy.wait_recv()
        piece = part(block, s)
        if n == 4:
            across.append([(mail.push(piece, piece, one, d), one), (mail.push(piece, piece, two, d), two)])
        else:
            across.append(
                [(mail.push(piece, piece, (s + m) % n, d), (s + n - m) % n) for m in range(1, n)]
            )
        waits.append(mail.push(piece, piece, s, mate))
    for group, block in zip(across, blocks):
        for at, (copy, source) in enumerate(group):
            copy.wait_recv()
            piece = part(block, source)
            if n == 4 and at == 0:
                group.append((mail.push(piece, piece, two, d), far))
            waits.append(mail.push(piece, piece, s, mate))
    for copy in waits:
        copy.wait_recv()
    mail.close()
    keep.wait()


def gather_all(shard, edges, n, nd):
    count = (nd // 2 - 1) * (1 + (n if n != 4 else 4) - 1 + n) + 4
    any_spec = pl.BlockSpec(memory_space=pl.ANY)
    shapes = [jax.ShapeDtypeStruct((nd,) + shard.shape, shard.dtype)]
    shapes += [jax.ShapeDtypeStruct(e.shape, e.dtype) for e in edges]
    return pl.pallas_call(
        functools.partial(gather_kernel, n, nd),
        out_shape=shapes,
        in_specs=[any_spec] * 4,
        out_specs=[any_spec] * 4,
        scratch_shapes=[
            pltpu.SemaphoreType.DMA((count,)),
            pltpu.SemaphoreType.DMA((count,)),
            pltpu.SemaphoreType.DMA,
        ],
        compiler_params=pltpu.CompilerParams(collective_id=0, has_side_effects=True),
    )(shard, *edges)


def reduce_kernel(n, nd, low, g_ref, e0, e1, e2, o_ref, t_ref, f0, f1, f2, held, ra, rb, mid, q_ref, rc, send, recv, own):
    s, d, one, two, far = places(n, nd)
    nz, core = nd // 2, d % 2
    z = d // 2
    mate = d + 1 - 2 * core
    quarter = o_ref.shape[0] // n

    def rows(q):
        return pl.ds(pl.multiple_of(q * quarter, TILE), quarter)

    greet(n, nd, s, d)
    mail = Mail(send, recv)
    order = list(range(1, nz)) + [0]
    first = [
        mail.push(g_ref.at[(z + k) % nz * 2 + 1 - core], ra.at[k], s, mate) for k in order
    ]
    second = []
    for k, copy in zip(order, first):
        copy.wait_recv()
        held[k] = g_ref[(z + k) % nz * 2 + core] + ra[k]
        if n == 4:
            second.append(
                [
                    mail.push(held.at[k, rows(far)], rb.at[k, 0], one, d),
                    mail.push(held.at[k, rows(one)], rb.at[k, 1], one, d),
                ]
            )
        else:
            second.append(
                [
                    mail.push(held.at[k, rows((s + m) % n)], rb.at[k, m - 1], (s + m) % n, d)
                    for m in range(1, n)
                ]
            )
    if n == 4:
        for k, group in zip(order, second):
            group[0].wait_recv()
            mid[k] = held[k, rows(two)] + rb[k, 0]
            group.append(mail.push(mid.at[k], rb.at[k, 2], two, d))
    edge = edge_sends(mail, n, s, d, (e0, e1, e2), (f0, f1, f2), 1)
    third = []
    for k, group in zip(order, second):
        total = held[k, rows(s)].astype(F32)
        for at in range(1 if n == 4 else 0, n - 1):
            group[at].wait_recv()
            total = total + rb[k, at].astype(F32)
        q_ref[k] = total.astype(BF16)
        if k:
            third.append(mail.push(q_ref.at[k], rc.at[k - 1], s, (z + k) % nz * 2 + core))
    total = q_ref[0].astype(F32)
    for k, copy in enumerate(third):
        copy.wait_recv()
        total = total + rc[k].astype(F32)
    o_ref[rows(s)] = total.astype(BF16)
    mine = o_ref.at[rows(s)]
    if n == 4:
        a, b = mail.push(mine, mine, one, d), mail.push(mine, mine, two, d)
        a.wait_recv()
        block = o_ref.at[rows(one)]
        last = [b, mail.push(block, block, two, d)]
    else:
        last = [mail.push(mine, mine, (s + m) % n, d) for m in range(1, n)]
    for copy in last:
        copy.wait_recv()
    table = o_ref.at[pl.ds(low, TILE)]
    keep = pltpu.make_async_copy(table, t_ref.at[d], own)
    keep.start()
    tables = [mail.push(table, t_ref.at[d], s, (d + m) % nd) for m in range(1, nd)]
    for copy in tables + edge:
        copy.wait_recv()
    mail.close()
    keep.wait()


def reduce_all(grads, edges, low, n, nd):
    nz = nd // 2
    rows, width = grads.shape[1:]
    quarter = rows // n
    count = nz * 4 + nz * n + n + nd + 8
    any_spec = pl.BlockSpec(memory_space=pl.ANY)
    vmem_spec = pl.BlockSpec(memory_space=pltpu.VMEM)
    shapes = [
        jax.ShapeDtypeStruct((rows, width), BF16),
        jax.ShapeDtypeStruct((nd, TILE, width), BF16),
    ]
    shapes += [jax.ShapeDtypeStruct(e.shape, e.dtype) for e in edges]
    return pl.pallas_call(
        functools.partial(reduce_kernel, n, nd, low),
        out_shape=shapes,
        in_specs=[vmem_spec] + [any_spec] * 3,
        out_specs=[vmem_spec, vmem_spec] + [any_spec] * 3,
        scratch_shapes=[
            pltpu.VMEM((nz, rows, width), BF16),
            pltpu.VMEM((nz, rows, width), BF16),
            pltpu.VMEM((nz, n - 1, quarter, width), BF16),
            pltpu.VMEM((nz, quarter, width), BF16),
            pltpu.VMEM((nz, quarter, width), BF16),
            pltpu.VMEM((nz - 1 if nz > 1 else 1, quarter, width), BF16),
            pltpu.SemaphoreType.DMA((count,)),
            pltpu.SemaphoreType.DMA((count,)),
            pltpu.SemaphoreType.DMA,
        ],
        compiler_params=pltpu.CompilerParams(
            collective_id=1, has_side_effects=True, vmem_limit_bytes=VMEM
        ),
    )(grads, *edges)


def to_windows(field):
    batch, rows, cols, width = field.shape
    return (
        field.reshape(batch, rows // SIDE, SIDE, cols // SIDE, SIDE, width)
        .transpose(0, 1, 3, 2, 4, 5)
        .reshape(-1, CELLS, width)
    )


def from_windows(blocks, batch, rows, cols):
    width = blocks.shape[-1]
    return (
        blocks.reshape(batch, rows // SIDE, cols // SIDE, SIDE, SIDE, width)
        .transpose(0, 1, 3, 2, 4, 5)
        .reshape(batch, rows, cols, width)
    )


def pad_windows(field):
    return jnp.pad(to_windows(field), ((0, 0), (0, ROWS - CELLS), (0, 0))).reshape(
        -1, field.shape[-1]
    )


def stack_heads(block, per):
    part = lax.broadcasted_iota(jnp.int32, block.shape, 1) // (block.shape[1] // per)
    return jnp.concatenate([jnp.where(part == j, block, jnp.zeros_like(block)) for j in range(per)], 0)


def merge_heads(tall, per):
    rows = tall.shape[0] // per
    part = lax.broadcasted_iota(jnp.int32, (rows, tall.shape[1]), 1) // (tall.shape[1] // per)
    total = jnp.where(part == 0, tall[:rows], 0.0)
    for j in range(1, per):
        total = jnp.where(part == j, tall[j * rows : (j + 1) * rows], total)
    return total


def dot_nt(left, right):
    return lax.dot_general(left, right, (((1,), (1,)), ((), ())), preferred_element_type=F32)


def dot_tn(left, right):
    return lax.dot_general(left, right, (((0,), (0,)), ((), ())), preferred_element_type=F32)


def dot_nn(left, right):
    return jnp.dot(left, right, preferred_element_type=F32)


def attend_kernel(scale, per, qkv_ref, bias_ref, mask_ref, o_ref, p_ref):
    dim = o_ref.shape[1]
    tall = per * PAIR
    mask = mask_ref[0]
    for g in range(dim // 128):
        at = slice(g * 128, (g + 1) * 128)
        band = slice(g * tall, (g + 1) * tall)
        q = stack_heads(qkv_ref[:, g * 128 : (g + 1) * 128], per)
        k = qkv_ref[:, dim + g * 128 : dim + (g + 1) * 128]
        v = qkv_ref[:, 2 * dim + g * 128 : 2 * dim + (g + 1) * 128]
        s = dot_nt(q, k) * scale + bias_ref[band, :]
        s = (s.reshape(per, PAIR, PAIR) + mask[None]).reshape(tall, PAIR)
        e = jnp.exp(s - jnp.max(s, -1, keepdims=True))
        p = (e * (1.0 / jnp.sum(e, -1, keepdims=True))).astype(BF16)
        p_ref[0, band, :] = p
        o_ref[:, at] = merge_heads(dot_nn(p, v), per).astype(BF16)


def attend_back_kernel(scale, per, qkv_ref, do_ref, p_ref, dqkv_ref, sum_ref):
    dim = do_ref.shape[1]
    tall = per * PAIR

    @pl.when(pl.program_id(0) == 0)
    def _():
        sum_ref[...] = jnp.zeros_like(sum_ref)

    for g in range(dim // 128):
        band = slice(g * tall, (g + 1) * tall)
        q = stack_heads(qkv_ref[:, g * 128 : (g + 1) * 128], per)
        k = qkv_ref[:, dim + g * 128 : dim + (g + 1) * 128]
        v = qkv_ref[:, 2 * dim + g * 128 : 2 * dim + (g + 1) * 128]
        do = stack_heads(do_ref[:, g * 128 : (g + 1) * 128], per)
        p = p_ref[0, band, :]
        pf = p.astype(F32)
        dp = dot_nt(do, v)
        dl = (pf * (dp - jnp.sum(dp * pf, -1, keepdims=True))).astype(BF16)
        sum_ref[band, :] += dl.astype(F32)
        dq = merge_heads(dot_nn(dl, k), per) * scale
        dk = dot_tn(dl, q) * scale
        dv = dot_tn(p, do)
        dqkv_ref[:, g * 128 : (g + 1) * 128] = dq.astype(BF16)
        dqkv_ref[:, dim + g * 128 : dim + (g + 1) * 128] = dk.astype(BF16)
        dqkv_ref[:, 2 * dim + g * 128 : 2 * dim + (g + 1) * 128] = dv.astype(BF16)


def attend(qkv, bias, mask, heads):
    rows, dim = qkv.shape[0], qkv.shape[1] // 3
    pairs = rows // PAIR
    per = 128 * heads // dim
    return pl.pallas_call(
        functools.partial(attend_kernel, (dim // heads) ** -0.5, per),
        grid=(pairs,),
        out_shape=(
            jax.ShapeDtypeStruct((rows, dim), BF16),
            jax.ShapeDtypeStruct((pairs, heads * PAIR, PAIR), BF16),
        ),
        in_specs=[
            pl.BlockSpec((PAIR, 3 * dim), lambda i: (i, 0)),
            pl.BlockSpec((heads * PAIR, PAIR), lambda i: (0, 0)),
            pl.BlockSpec((1, PAIR, PAIR), lambda i: (i, 0, 0)),
        ],
        out_specs=(
            pl.BlockSpec((PAIR, dim), lambda i: (i, 0)),
            pl.BlockSpec((1, heads * PAIR, PAIR), lambda i: (i, 0, 0)),
        ),
        compiler_params=pltpu.CompilerParams(vmem_limit_bytes=VMEM),
        cost_estimate=pl.CostEstimate(
            flops=4 * rows * heads * PAIR * 128, bytes_accessed=rows * dim * 8, transcendentals=rows * heads * 128
        ),
    )(qkv, bias, mask)


def attend_back(qkv, grad, probs, heads):
    rows, dim = grad.shape
    pairs = rows // PAIR
    per = 128 * heads // dim
    return pl.pallas_call(
        functools.partial(attend_back_kernel, (dim // heads) ** -0.5, per),
        grid=(pairs,),
        out_shape=(
            jax.ShapeDtypeStruct((rows, 3 * dim), BF16),
            jax.ShapeDtypeStruct((heads * PAIR, PAIR), F32),
        ),
        in_specs=[
            pl.BlockSpec((PAIR, 3 * dim), lambda i: (i, 0)),
            pl.BlockSpec((PAIR, dim), lambda i: (i, 0)),
            pl.BlockSpec((1, heads * PAIR, PAIR), lambda i: (i, 0, 0)),
        ],
        out_specs=(
            pl.BlockSpec((PAIR, 3 * dim), lambda i: (i, 0)),
            pl.BlockSpec((heads * PAIR, PAIR), lambda i: (0, 0)),
        ),
        compiler_params=pltpu.CompilerParams(vmem_limit_bytes=VMEM),
        cost_estimate=pl.CostEstimate(
            flops=8 * rows * heads * PAIR * 128, bytes_accessed=rows * dim * 16, transcendentals=0
        ),
    )(qkv, grad, probs)


def normalize(values):
    center = values - jnp.mean(values, -1, keepdims=True)
    scaled = lax.rsqrt(jnp.mean(center * center, -1, keepdims=True) + 1e-05)
    return center * scaled, scaled


def normalize_back(grad, unit, scaled, gain):
    inner = grad * gain
    return scaled * (
        inner
        - jnp.mean(inner, -1, keepdims=True)
        - unit * jnp.mean(inner * unit, -1, keepdims=True)
    )


def local(
    tokens,
    cotangent,
    norm1_gain,
    norm1_bias,
    qkv_weight,
    query_bias,
    value_bias,
    proj_weight,
    proj_bias,
    norm2_gain,
    norm2_bias,
    fc1_weight,
    fc1_bias,
    fc2_weight,
    fc2_bias,
    bias_table,
    region_ids,
    rel_index,
):
    batch = tokens.shape[0]
    dim = tokens.shape[-1]
    heads = bias_table.shape[1]
    image_rows, image_cols = region_ids.shape
    seq_count = lax.axis_size("seq")
    tile_rows = image_rows // 2
    tile_cols = image_cols * 2 // seq_count
    place = lax.axis_index("seq")

    count = lax.axis_size("dp")
    share = dim // count
    wide = fc1_weight.shape[1] // dim

    smalls = [
        norm1_gain, norm1_bias, query_bias, value_bias, proj_bias, norm2_gain, norm2_bias, fc2_bias, fc1_bias,
    ]
    low = share * (4 + 2 * wide)
    total_rows = -(-(low + TILE) // (TILE * seq_count)) * TILE * seq_count
    tail = total_rows - low
    short = jnp.concatenate(smalls)
    small_size = short.shape[0]
    short = jnp.pad(short, (0, tail * dim - small_size)).reshape(tail, dim)

    def columns(matrix):
        return [matrix[:, at : at + dim] for at in range(0, matrix.shape[1], dim)]

    shard = jnp.concatenate(
        columns(qkv_weight) + [proj_weight] + columns(fc1_weight) + [fc2_weight, short], 0
    )
    tile = tokens.reshape(batch, tile_rows, tile_cols, dim)
    grad_tile = cotangent.reshape(batch, tile_rows, tile_cols, dim)
    edges = [edges_ahead(tile), edges_ahead(grad_tile)]
    gathered, *blocks = gather_all(shard, pack_edges(edges), seq_count, count)
    blocks = unpack_edges(blocks, edges)

    def matrix_of(at, blocks_wide):
        parts = [
            gathered[:, at + j * share : at + (j + 1) * share].reshape(dim, dim) for j in range(blocks_wide)
        ]
        return parts[0] if blocks_wide == 1 else jnp.concatenate(parts, 1)

    qkv_full = matrix_of(0, 3)
    proj_full = matrix_of(3 * share, 1)
    fc1_full = matrix_of(4 * share, wide)
    fc2_full = gathered[:, (4 + wide) * share : low].reshape(-1, dim)
    small_all = gathered[:, low:].reshape(count, -1)
    full, at = [], 0
    for v in smalls:
        full.append(small_all[:, at : at + v.shape[0]].reshape(-1).astype(F32))
        at += v.shape[0]
    gain_one, shift_one, qbias, vbias, pbias, gain_two, shift_two, fc2b, fc1b = full

    regions = lax.dynamic_slice(
        region_ids, (place % 2 * tile_rows, place // 2 * tile_cols), (tile_rows, tile_cols)
    )
    region_win = to_windows(regions[None, :, :, None])[:, :, 0]
    mask = jnp.where(region_win[:, :, None] == region_win[:, None, :], 0.0, -100.0).astype(F32)
    mask = jnp.tile(mask, (batch, 1, 1))
    shut = -1e30
    mask = jnp.pad(mask, ((0, 0), (0, 0), (0, ROWS - CELLS)), constant_values=shut)
    mask = jnp.pad(mask, ((0, 0), (0, ROWS - CELLS), (0, 0)))
    mask = mask.at[:, CELLS:, CELLS:].set(shut)
    mask = mask.reshape(-1, 2, ROWS, ROWS)
    other = jnp.full_like(mask[:, 0], shut)
    mask = jnp.concatenate(
        [jnp.concatenate([mask[:, 0], other], 2), jnp.concatenate([other, mask[:, 1]], 2)], 1
    )
    onehot = (
        rel_index.reshape(-1)[:, None] == jnp.arange(bias_table.shape[0], dtype=jnp.int32)[None, :]
    ).astype(F32)
    bias = jnp.dot(onehot, bias_table, precision=HIGHEST).reshape(CELLS, CELLS, heads).transpose(2, 0, 1)
    bias = jnp.pad(bias, ((0, 0), (0, ROWS - CELLS), (0, ROWS - CELLS)))
    bias = jnp.tile(bias, (1, 2, 2)).reshape(heads * PAIR, PAIR)

    source = pad_windows(join_ahead(tile, *blocks[0]))
    grad_out = pad_windows(join_ahead(grad_tile, *blocks[1]))
    source = source.astype(F32)

    unit_one, scaled_one = normalize(source)
    first = (unit_one * gain_one + shift_one).astype(BF16)
    qkv_bias = jnp.concatenate([qbias, jnp.zeros((dim,), F32), vbias])
    qkv = (dot_nn(first, qkv_full) + qkv_bias).astype(BF16)
    mixed, probs = attend(qkv, bias, mask, heads)
    resid = source + dot_nn(mixed, proj_full) + pbias
    unit_two, scaled_two = normalize(resid)
    second = (unit_two * gain_two + shift_two).astype(BF16)
    before = dot_nn(second, fc1_full) + fc1b
    normal_cdf = 0.5 * (1.0 + lax.erf(before * 0.7071067811865476))
    hidden = (before * normal_cdf).astype(BF16)
    output = (resid + dot_nn(hidden, fc2_full) + fc2b).astype(BF16)

    def to_tile(field):
        field = field.reshape(-1, ROWS, dim)[:, :CELLS]
        return from_windows(field, batch, tile_rows, tile_cols)

    output = to_tile(output)

    grad_fc2 = dot_tn(hidden, grad_out)
    grad_fc2b = jnp.sum(grad_out.astype(F32), 0)
    grad_hidden = dot_nt(grad_out, fc2_full)
    normal_pdf = jnp.exp(-0.5 * before * before) * 0.3989422804014327
    grad_before = (grad_hidden * (normal_cdf + before * normal_pdf)).astype(BF16)
    grad_fc1 = dot_tn(second, grad_before)
    grad_fc1b = jnp.sum(grad_before.astype(F32), 0)
    grad_second = dot_nt(grad_before, fc1_full)
    grad_gain2 = jnp.sum(grad_second * unit_two, 0)
    grad_shift2 = jnp.sum(grad_second, 0)
    grad_resid = grad_out.astype(F32) + normalize_back(grad_second, unit_two, scaled_two, gain_two)
    grad_pbias = jnp.sum(grad_resid, 0)
    grad_branch = grad_resid.astype(BF16)
    grad_proj = dot_tn(mixed, grad_branch)
    grad_mixed = dot_nt(grad_branch, proj_full).astype(BF16)
    grad_qkv_rows, score_sum = attend_back(qkv, grad_mixed, probs, heads)
    score_sum = score_sum.reshape(heads, PAIR, PAIR)
    score_sum = score_sum[:, :CELLS, :CELLS] + score_sum[:, ROWS : ROWS + CELLS, ROWS : ROWS + CELLS]
    grad_table = jnp.dot(
        onehot.T, score_sum.transpose(1, 2, 0).reshape(-1, heads), precision=HIGHEST
    )
    grad_qkv = dot_tn(first, grad_qkv_rows)
    grad_qkvb = jnp.sum(grad_qkv_rows.astype(F32), 0)
    grad_first = dot_nt(grad_qkv_rows, qkv_full).astype(BF16).astype(F32)
    grad_gain1 = jnp.sum(grad_first * unit_one, 0)
    grad_shift1 = jnp.sum(grad_first, 0)
    input_grad = normalize_back(grad_first, unit_one, scaled_one, gain_one) + grad_resid
    input_grad = to_tile(input_grad.astype(BF16))

    def rows_of(matrix):
        return [m.reshape(count, share, dim) for m in columns(matrix.astype(BF16))]

    vectors = [
        grad_gain1, grad_shift1, grad_qkvb[:dim], grad_qkvb[2 * dim :], grad_pbias, grad_gain2,
        grad_shift2, grad_fc2b, grad_fc1b,
    ]
    table_row = -(-small_size // dim)
    table_size = -(-grad_table.size // count)
    short = jnp.concatenate([v.reshape(count, -1) for v in vectors], 1)
    short = jnp.pad(short, ((0, 0), (0, table_row * dim - small_size)))
    spread = jnp.pad(grad_table.reshape(-1), (0, table_size * count - grad_table.size))
    short = jnp.concatenate([short, spread.reshape(count, -1)], 1)
    short = jnp.pad(short, ((0, 0), (0, tail * dim - short.shape[1]))).reshape(count, tail, dim)
    grads = jnp.concatenate(
        rows_of(grad_qkv)
        + rows_of(grad_proj)
        + rows_of(grad_fc1)
        + [grad_fc2.astype(BF16).reshape(count, -1, dim), short.astype(BF16)],
        1,
    )
    edges = [edges_behind(output), edges_behind(input_grad)]
    summed, tables, *blocks = reduce_all(grads, pack_edges(edges), low, seq_count, count)
    blocks = unpack_edges(blocks, edges)
    output = join_behind(output, *blocks[0]).reshape(tokens.shape)
    input_grad = join_behind(input_grad, *blocks[1]).reshape(tokens.shape)
    summed = summed.astype(F32)

    def matrix_sum(at, blocks_wide):
        parts = [summed[at + j * share : at + (j + 1) * share] for j in range(blocks_wide)]
        return parts[0] if blocks_wide == 1 else jnp.concatenate(parts, 1)

    sum_qkv = matrix_sum(0, 3)
    sum_proj = matrix_sum(3 * share, 1)
    sum_fc1 = matrix_sum(4 * share, wide)
    sum_fc2 = summed[(4 + wide) * share : low]
    short = summed[low:].reshape(-1)
    owned, at = [], 0
    for v in vectors:
        size = v.shape[0] // count
        owned.append(short[at : at + size])
        at += size
    table_total = tables.astype(F32)[:, table_row:].reshape(count, -1)[:, :table_size]
    table_total = table_total.reshape(-1)[: bias_table.size].reshape(bias_table.shape)
    s_gain1, s_shift1, s_qb, s_vb, s_pb, s_gain2, s_shift2, s_fc2b, s_fc1b = owned
    return (
        output,
        input_grad,
        s_gain1,
        s_shift1,
        sum_qkv,
        s_qb,
        s_vb,
        sum_proj,
        s_pb,
        s_gain2,
        s_shift2,
        sum_fc1,
        s_fc1b,
        sum_fc2,
        s_fc2b,
        table_total,
    )


def solution(mesh):
    rows, vector, matrix, whole = P("dp", "seq", None, None), P("dp"), P("dp", None), P()
    params = (
        vector, vector, matrix, vector, vector, matrix, vector, vector, vector, matrix, vector, matrix, vector,
    )
    in_specs = (rows, rows) + params + (whole, whole, whole)
    out_specs = (rows, rows) + params + (whole,)
    return jax.shard_map(local, mesh=mesh, in_specs=in_specs, out_specs=out_specs, check_vma=False)
```

```python
import functools

import jax
import jax.numpy as jnp
from jax import lax
from jax.experimental import pallas as pl
from jax.experimental.pallas import tpu as pltpu
from jax.sharding import PartitionSpec as P

HIGHEST = lax.Precision.HIGHEST
F32 = jnp.float32
BF16 = jnp.bfloat16
SIDE = 7
CELLS = SIDE * SIDE
ROWS = 56
PAIR = 2 * ROWS
VMEM = 56 * 1024 * 1024


MESH = pl.DeviceIdType.MESH
TILE = 16
STEP = 3


def edges_ahead(field):
    return field[:, :STEP, STEP:], field[:, STEP:, :STEP], field[:, :STEP, :STEP]


def edges_behind(field):
    return field[:, -STEP:, :-STEP], field[:, :-STEP, -STEP:], field[:, -STEP:, -STEP:]


def join_ahead(field, below, beside, corner):
    top = jnp.concatenate([field[:, STEP:, STEP:], beside], 2)
    return jnp.concatenate([top, jnp.concatenate([below, corner], 2)], 1)


def join_behind(field, above, beside, corner):
    low = jnp.concatenate([beside, field[:, :-STEP, :-STEP]], 2)
    return jnp.concatenate([jnp.concatenate([corner, above], 2), low], 1)


def pack_edges(edges):
    packed = []
    for blocks in zip(*edges):
        rows = jnp.concatenate([b.reshape(-1, b.shape[-1]) for b in blocks], 0)
        packed.append(jnp.pad(rows, ((0, -rows.shape[0] % TILE), (0, 0))))
    return packed


def unpack_edges(packed, edges):
    fields = [[] for _ in edges]
    for rows, blocks in zip(packed, zip(*edges)):
        at = 0
        for field, b in zip(fields, blocks):
            size = b.size // b.shape[-1]
            field.append(rows[at : at + size].reshape(b.shape))
            at += size
    return fields


class Mail:
    def __init__(self, send, recv):
        self.send, self.recv, self.used, self.open = send, recv, 0, []

    def push(self, src, dst, seq, dp):
        copy = pltpu.make_async_remote_copy(
            src_ref=src,
            dst_ref=dst,
            send_sem=self.send.at[self.used],
            recv_sem=self.recv.at[self.used],
            device_id=(seq, dp),
            device_id_type=MESH,
        )
        copy.start()
        self.used += 1
        self.open.append(copy)
        return copy

    def close(self):
        for copy in self.open:
            copy.wait_send()


def places(n, nd):
    s, d = lax.axis_index("seq"), lax.axis_index("dp")
    core = d % 2
    row = s + 1 - 2 * (s % 2)
    col = (s + 2) % n
    one = (1 - core) * row + core * col
    two = core * row + (1 - core) * col
    return s, d, one, two, (s // 2 * 2 + 2) % n + 1 - s % 2


def greet(n, nd, s, d):
    barrier = pltpu.get_barrier_semaphore()
    for m in range(1, n):
        pl.semaphore_signal(barrier, inc=1, device_id=((s + m) % n, d), device_id_type=MESH)
    for m in range(1, nd):
        pl.semaphore_signal(barrier, inc=1, device_id=(s, (d + m) % nd), device_id_type=MESH)
    pl.semaphore_wait(barrier, n - 1 + nd - 1)


def edge_sends(mail, n, s, d, src, dst, cols):
    row = s + 1 - 2 * (s % 2)
    col = (s + 2 * cols + n) % n
    return [
        mail.push(src[0], dst[0], row, d),
        mail.push(src[1], dst[1], col, d),
        mail.push(src[2], dst[2], col + 1 - 2 * (col % 2), d),
    ]


def gather_kernel(n, nd, w_ref, e0, e1, e2, o_ref, f0, f1, f2, send, recv, own):
    s, d, one, two, far = places(n, nd)
    nz, core = nd // 2, d % 2
    z = d // 2
    mate = d + 1 - 2 * core
    quarter = w_ref.shape[0] // n

    def part(block, q, span):
        return o_ref.at[block, pl.ds(pl.multiple_of(q * quarter + span[0], TILE), span[1])]

    greet(n, nd, s, d)
    mail = Mail(send, recv)
    keep = pltpu.make_async_copy(w_ref, o_ref.at[d], own)
    keep.start()
    spans = chunks(quarter)
    along = []
    for span in spans:
        mine = w_ref.at[pl.ds(pl.multiple_of(s * quarter + span[0], TILE), span[1])]
        for k in range(1, nz):
            copy = mail.push(mine, part(d, s, span), s, (z + k) % nz * 2 + core)
            along.append((copy, (z + nz - k) % nz * 2 + core, span))
    waits = edge_sends(mail, n, s, d, (e0, e1, e2), (f0, f1, f2), -1)
    waits.append(mail.push(w_ref, o_ref.at[d], s, mate))

    def spread(group):
        across = []
        for copy, block, span in group:
            copy.wait_recv()
            piece = part(block, s, span)
            peers = [(one, one), (two, two)]
            if n != 4:
                peers = [((s + m) % n, (s + n - m) % n) for m in range(1, n)]
            sent = [(mail.push(piece, piece, to, d), source) for to, source in peers]
            across.append((sent, block, span))
            waits.append(mail.push(piece, piece, s, mate))
        return across

    def relay(across):
        for sent, block, span in across:
            for at, (copy, source) in enumerate(sent):
                copy.wait_recv()
                piece = part(block, source, span)
                if n == 4 and at == 0:
                    sent.append((mail.push(piece, piece, two, d), far))
                waits.append(mail.push(piece, piece, s, mate))

    before = []
    for at in range(len(spans)):
        after = spread(along[at * (nz - 1) : (at + 1) * (nz - 1)])
        relay(before)
        before = after
    relay(before)
    for copy in waits:
        copy.wait_recv()
    mail.close()
    keep.wait()


def chunks(rows):
    tiles = rows // TILE
    cuts = sorted({0, tiles // 3, 2 * tiles // 3, tiles})
    return [(a * TILE, (b - a) * TILE) for a, b in zip(cuts, cuts[1:])]


def gather_all(shard, edges, n, nd):
    count = len(chunks(shard.shape[0] // n)) * (nd // 2 - 1) * 2 * n + 4
    any_spec = pl.BlockSpec(memory_space=pl.ANY)
    shapes = [jax.ShapeDtypeStruct((nd,) + shard.shape, shard.dtype)]
    shapes += [jax.ShapeDtypeStruct(e.shape, e.dtype) for e in edges]
    return pl.pallas_call(
        functools.partial(gather_kernel, n, nd),
        out_shape=shapes,
        in_specs=[any_spec] * 4,
        out_specs=[any_spec] * 4,
        scratch_shapes=[
            pltpu.SemaphoreType.DMA((count,)),
            pltpu.SemaphoreType.DMA((count,)),
            pltpu.SemaphoreType.DMA,
        ],
        compiler_params=pltpu.CompilerParams(collective_id=0, has_side_effects=True),
    )(shard, *edges)


def reduce_kernel(n, nd, low, g_ref, e0, e1, e2, o_ref, t_ref, f0, f1, f2, held, ra, rb, mid, q_ref, rc, send, recv, own):
    s, d, one, two, far = places(n, nd)
    nz, core = nd // 2, d % 2
    z = d // 2
    mate = d + 1 - 2 * core
    quarter = o_ref.shape[0] // n

    def rows(q):
        return pl.ds(pl.multiple_of(q * quarter, TILE), quarter)

    greet(n, nd, s, d)
    mail = Mail(send, recv)
    order = list(range(1, nz)) + [0]
    first = [
        mail.push(g_ref.at[(z + k) % nz * 2 + 1 - core], ra.at[k], s, mate) for k in order
    ]
    second, third = {}, []

    def across(k, copy):
        copy.wait_recv()
        held[k] = g_ref[(z + k) % nz * 2 + core] + ra[k]
        peers = [(far, one), (one, one)]
        if n != 4:
            peers = [((s + m) % n, (s + m) % n) for m in range(1, n)]
        second[k] = [
            mail.push(held.at[k, rows(q)], rb.at[k, at], to, d) for at, (q, to) in enumerate(peers)
        ]

    def relay(k):
        if n == 4:
            second[k][0].wait_recv()
            mid[k] = held[k, rows(two)] + rb[k, 0]
            second[k].append(mail.push(mid.at[k], rb.at[k, 2], two, d))

    def along(k):
        total = held[k, rows(s)].astype(F32)
        for at in range(1 if n == 4 else 0, n - 1):
            second[k][at].wait_recv()
            total = total + rb[k, at].astype(F32)
        q_ref[k] = total.astype(BF16)
        if k:
            third.append(mail.push(q_ref.at[k], rc.at[k - 1], s, (z + k) % nz * 2 + core))

    for step in range(nz + 2):
        if step < nz:
            across(order[step], first[step])
        if 0 <= step - 1 < nz:
            relay(order[step - 1])
        if 0 <= step - 2:
            along(order[step - 2])
    edge = edge_sends(mail, n, s, d, (e0, e1, e2), (f0, f1, f2), 1)
    total = q_ref[0].astype(F32)
    for k, copy in enumerate(third):
        copy.wait_recv()
        total = total + rc[k].astype(F32)
    o_ref[rows(s)] = total.astype(BF16)
    mine = o_ref.at[rows(s)]
    if n == 4:
        a, b = mail.push(mine, mine, one, d), mail.push(mine, mine, two, d)
        a.wait_recv()
        block = o_ref.at[rows(one)]
        last = [b, mail.push(block, block, two, d)]
    else:
        last = [mail.push(mine, mine, (s + m) % n, d) for m in range(1, n)]
    for copy in last:
        copy.wait_recv()
    table = o_ref.at[pl.ds(low, TILE)]
    keep = pltpu.make_async_copy(table, t_ref.at[d], own)
    keep.start()
    tables = [mail.push(table, t_ref.at[d], s, (d + m) % nd) for m in range(1, nd)]
    for copy in tables + edge:
        copy.wait_recv()
    mail.close()
    keep.wait()


def reduce_all(grads, edges, low, n, nd):
    nz = nd // 2
    rows, width = grads.shape[1:]
    quarter = rows // n
    count = nz * 4 + nz * n + n + nd + 8
    any_spec = pl.BlockSpec(memory_space=pl.ANY)
    vmem_spec = pl.BlockSpec(memory_space=pltpu.VMEM)
    shapes = [
        jax.ShapeDtypeStruct((rows, width), BF16),
        jax.ShapeDtypeStruct((nd, TILE, width), BF16),
    ]
    shapes += [jax.ShapeDtypeStruct(e.shape, e.dtype) for e in edges]
    return pl.pallas_call(
        functools.partial(reduce_kernel, n, nd, low),
        out_shape=shapes,
        in_specs=[vmem_spec] + [any_spec] * 3,
        out_specs=[vmem_spec, vmem_spec] + [any_spec] * 3,
        scratch_shapes=[
            pltpu.VMEM((nz, rows, width), BF16),
            pltpu.VMEM((nz, rows, width), BF16),
            pltpu.VMEM((nz, n - 1, quarter, width), BF16),
            pltpu.VMEM((nz, quarter, width), BF16),
            pltpu.VMEM((nz, quarter, width), BF16),
            pltpu.VMEM((nz - 1 if nz > 1 else 1, quarter, width), BF16),
            pltpu.SemaphoreType.DMA((count,)),
            pltpu.SemaphoreType.DMA((count,)),
            pltpu.SemaphoreType.DMA,
        ],
        compiler_params=pltpu.CompilerParams(
            collective_id=1, has_side_effects=True, vmem_limit_bytes=VMEM
        ),
    )(grads, *edges)


def to_windows(field):
    batch, rows, cols, width = field.shape
    return (
        field.reshape(batch, rows // SIDE, SIDE, cols // SIDE, SIDE, width)
        .transpose(0, 1, 3, 2, 4, 5)
        .reshape(-1, CELLS, width)
    )


def from_windows(blocks, batch, rows, cols):
    width = blocks.shape[-1]
    return (
        blocks.reshape(batch, rows // SIDE, cols // SIDE, SIDE, SIDE, width)
        .transpose(0, 1, 3, 2, 4, 5)
        .reshape(batch, rows, cols, width)
    )


def pad_windows(field):
    return jnp.pad(to_windows(field), ((0, 0), (0, ROWS - CELLS), (0, 0))).reshape(
        -1, field.shape[-1]
    )


def stack_heads(block, per):
    part = lax.broadcasted_iota(jnp.int32, block.shape, 1) // (block.shape[1] // per)
    return jnp.concatenate([jnp.where(part == j, block, jnp.zeros_like(block)) for j in range(per)], 0)


def merge_heads(tall, per):
    rows = tall.shape[0] // per
    part = lax.broadcasted_iota(jnp.int32, (rows, tall.shape[1]), 1) // (tall.shape[1] // per)
    total = jnp.where(part == 0, tall[:rows], 0.0)
    for j in range(1, per):
        total = jnp.where(part == j, tall[j * rows : (j + 1) * rows], total)
    return total


def dot_nt(left, right):
    return lax.dot_general(left, right, (((1,), (1,)), ((), ())), preferred_element_type=F32)


def dot_tn(left, right):
    return lax.dot_general(left, right, (((0,), (0,)), ((), ())), preferred_element_type=F32)


def dot_nn(left, right):
    return jnp.dot(left, right, preferred_element_type=F32)


def attend_kernel(scale, per, qkv_ref, bias_ref, mask_ref, o_ref, p_ref):
    dim = o_ref.shape[1]
    tall = per * PAIR
    mask = mask_ref[0]
    for g in range(dim // 128):
        at = slice(g * 128, (g + 1) * 128)
        band = slice(g * tall, (g + 1) * tall)
        q = stack_heads(qkv_ref[:, g * 128 : (g + 1) * 128], per)
        k = qkv_ref[:, dim + g * 128 : dim + (g + 1) * 128]
        v = qkv_ref[:, 2 * dim + g * 128 : 2 * dim + (g + 1) * 128]
        s = dot_nt(q, k) * scale
        s = s.reshape(per, 2, ROWS, PAIR) + bias_ref[g * per : (g + 1) * per][:, None]
        s = (s.reshape(per, PAIR, PAIR) + mask[None]).reshape(tall, PAIR)
        e = jnp.exp(s - jnp.max(s, -1, keepdims=True))
        p = (e * (1.0 / jnp.sum(e, -1, keepdims=True))).astype(BF16)
        p_ref[0, band, :] = p
        o_ref[:, at] = merge_heads(dot_nn(p, v), per).astype(BF16)


def attend_back_kernel(scale, per, qkv_ref, do_ref, p_ref, dqkv_ref, sum_ref):
    dim = do_ref.shape[1]
    tall = per * PAIR

    @pl.when(pl.program_id(0) == 0)
    def _():
        sum_ref[...] = jnp.zeros_like(sum_ref)

    for g in range(dim // 128):
        band = slice(g * tall, (g + 1) * tall)
        q = stack_heads(qkv_ref[:, g * 128 : (g + 1) * 128], per)
        k = qkv_ref[:, dim + g * 128 : dim + (g + 1) * 128]
        v = qkv_ref[:, 2 * dim + g * 128 : 2 * dim + (g + 1) * 128]
        do = stack_heads(do_ref[:, g * 128 : (g + 1) * 128], per)
        p = p_ref[0, band, :]
        pf = p.astype(F32)
        dp = dot_nt(do, v)
        dl = (pf * (dp - jnp.sum(dp * pf, -1, keepdims=True))).astype(BF16)
        sum_ref[band, :] += dl.astype(F32)
        dq = merge_heads(dot_nn(dl, k), per) * scale
        dk = dot_tn(dl, q) * scale
        dv = dot_tn(p, do)
        dqkv_ref[:, g * 128 : (g + 1) * 128] = dq.astype(BF16)
        dqkv_ref[:, dim + g * 128 : dim + (g + 1) * 128] = dk.astype(BF16)
        dqkv_ref[:, 2 * dim + g * 128 : 2 * dim + (g + 1) * 128] = dv.astype(BF16)


def attend(qkv, bias, mask, heads):
    rows, dim = qkv.shape[0], qkv.shape[1] // 3
    pairs = rows // PAIR
    per = 128 * heads // dim
    return pl.pallas_call(
        functools.partial(attend_kernel, (dim // heads) ** -0.5, per),
        grid=(pairs,),
        out_shape=(
            jax.ShapeDtypeStruct((rows, dim), BF16),
            jax.ShapeDtypeStruct((pairs, heads * PAIR, PAIR), BF16),
        ),
        in_specs=[
            pl.BlockSpec((PAIR, 3 * dim), lambda i: (i, 0)),
            pl.BlockSpec((heads, ROWS, PAIR), lambda i: (0, 0, 0)),
            pl.BlockSpec((1, PAIR, PAIR), lambda i: (i, 0, 0)),
        ],
        out_specs=(
            pl.BlockSpec((PAIR, dim), lambda i: (i, 0)),
            pl.BlockSpec((1, heads * PAIR, PAIR), lambda i: (i, 0, 0)),
        ),
        compiler_params=pltpu.CompilerParams(vmem_limit_bytes=VMEM),
        cost_estimate=pl.CostEstimate(
            flops=4 * rows * heads * PAIR * 128, bytes_accessed=rows * dim * 8, transcendentals=rows * heads * 128
        ),
    )(qkv, bias, mask)


def attend_back(qkv, grad, probs, heads):
    rows, dim = grad.shape
    pairs = rows // PAIR
    per = 128 * heads // dim
    return pl.pallas_call(
        functools.partial(attend_back_kernel, (dim // heads) ** -0.5, per),
        grid=(pairs,),
        out_shape=(
            jax.ShapeDtypeStruct((rows, 3 * dim), BF16),
            jax.ShapeDtypeStruct((heads * PAIR, PAIR), F32),
        ),
        in_specs=[
            pl.BlockSpec((PAIR, 3 * dim), lambda i: (i, 0)),
            pl.BlockSpec((PAIR, dim), lambda i: (i, 0)),
            pl.BlockSpec((1, heads * PAIR, PAIR), lambda i: (i, 0, 0)),
        ],
        out_specs=(
            pl.BlockSpec((PAIR, 3 * dim), lambda i: (i, 0)),
            pl.BlockSpec((heads * PAIR, PAIR), lambda i: (0, 0)),
        ),
        compiler_params=pltpu.CompilerParams(vmem_limit_bytes=VMEM),
        cost_estimate=pl.CostEstimate(
            flops=8 * rows * heads * PAIR * 128, bytes_accessed=rows * dim * 16, transcendentals=0
        ),
    )(qkv, grad, probs)


def normalize(values):
    center = values - jnp.mean(values, -1, keepdims=True)
    scaled = lax.rsqrt(jnp.mean(center * center, -1, keepdims=True) + 1e-05)
    return center * scaled, scaled


def normalize_back(grad, unit, scaled, gain):
    inner = grad * gain
    return scaled * (
        inner
        - jnp.mean(inner, -1, keepdims=True)
        - unit * jnp.mean(inner * unit, -1, keepdims=True)
    )


def local(
    tokens,
    cotangent,
    norm1_gain,
    norm1_bias,
    qkv_weight,
    query_bias,
    value_bias,
    proj_weight,
    proj_bias,
    norm2_gain,
    norm2_bias,
    fc1_weight,
    fc1_bias,
    fc2_weight,
    fc2_bias,
    bias_table,
    region_ids,
    rel_index,
):
    batch = tokens.shape[0]
    dim = tokens.shape[-1]
    heads = bias_table.shape[1]
    image_rows, image_cols = region_ids.shape
    seq_count = lax.axis_size("seq")
    tile_rows = image_rows // 2
    tile_cols = image_cols * 2 // seq_count
    place = lax.axis_index("seq")

    count = lax.axis_size("dp")
    share = dim // count
    wide = fc1_weight.shape[1] // dim

    smalls = [
        norm1_gain, norm1_bias, query_bias, value_bias, proj_bias, norm2_gain, norm2_bias, fc2_bias, fc1_bias,
    ]
    low = share * (4 + 2 * wide)
    total_rows = -(-(low + TILE) // (TILE * seq_count)) * TILE * seq_count
    tail = total_rows - low
    short = jnp.concatenate(smalls)
    small_size = short.shape[0]
    short = jnp.pad(short, (0, tail * dim - small_size)).reshape(tail, dim)

    def columns(matrix):
        return [matrix[:, at : at + dim] for at in range(0, matrix.shape[1], dim)]

    shard = jnp.concatenate(
        columns(qkv_weight) + [proj_weight] + columns(fc1_weight) + [fc2_weight, short], 0
    )
    tile = tokens.reshape(batch, tile_rows, tile_cols, dim)
    grad_tile = cotangent.reshape(batch, tile_rows, tile_cols, dim)
    edges = [edges_ahead(tile), edges_ahead(grad_tile)]
    gathered, *blocks = gather_all(shard, pack_edges(edges), seq_count, count)
    blocks = unpack_edges(blocks, edges)

    def matrix_of(at, blocks_wide):
        parts = [
            gathered[:, at + j * share : at + (j + 1) * share].reshape(dim, dim) for j in range(blocks_wide)
        ]
        return parts[0] if blocks_wide == 1 else jnp.concatenate(parts, 1)

    qkv_full = matrix_of(0, 3)
    proj_full = matrix_of(3 * share, 1)
    fc1_full = matrix_of(4 * share, wide)
    fc2_full = gathered[:, (4 + wide) * share : low].reshape(-1, dim)
    small_all = gathered[:, low:].reshape(count, -1)
    full, at = [], 0
    for v in smalls:
        full.append(small_all[:, at : at + v.shape[0]].reshape(-1).astype(F32))
        at += v.shape[0]
    gain_one, shift_one, qbias, vbias, pbias, gain_two, shift_two, fc2b, fc1b = full

    regions = lax.dynamic_slice(
        region_ids, (place % 2 * tile_rows, place // 2 * tile_cols), (tile_rows, tile_cols)
    )
    region_win = to_windows(regions[None, :, :, None])[:, :, 0]
    region_win = jnp.pad(region_win, ((0, 0), (0, ROWS - CELLS)), constant_values=-1)
    region_win = jnp.tile(region_win.reshape(-1, PAIR), (batch, 1))
    half = jnp.arange(PAIR, dtype=jnp.int32) // ROWS
    mask = jnp.where(region_win[:, :, None] == region_win[:, None, :], 0.0, -100.0).astype(F32)
    shut = (half[:, None] != half[None, :])[None] | (region_win < 0)[:, None, :]
    mask = jnp.where(shut, -1e30, mask)
    index = jnp.pad(rel_index, ((0, ROWS - CELLS), (0, ROWS - CELLS)))
    names = jnp.arange(bias_table.shape[0], dtype=jnp.int32)
    onehot = (index.reshape(-1)[:, None] == names[None, :]).astype(F32)
    twice = jnp.tile(index, (1, 2)).reshape(-1)
    bias = jnp.dot(
        bias_table.T, (names[:, None] == twice[None, :]).astype(F32), precision=HIGHEST
    ).reshape(heads, ROWS, PAIR)

    source = pad_windows(join_ahead(tile, *blocks[0]))
    grad_out = pad_windows(join_ahead(grad_tile, *blocks[1]))
    source = source.astype(F32)

    unit_one, scaled_one = normalize(source)
    first = (unit_one * gain_one + shift_one).astype(BF16)
    qkv_bias = jnp.concatenate([qbias, jnp.zeros((dim,), F32), vbias])
    qkv = (dot_nn(first, qkv_full) + qkv_bias).astype(BF16)
    mixed, probs = attend(qkv, bias, mask, heads)
    resid = source + dot_nn(mixed, proj_full) + pbias
    unit_two, scaled_two = normalize(resid)
    second = (unit_two * gain_two + shift_two).astype(BF16)
    before = dot_nn(second, fc1_full) + fc1b
    normal_cdf = 0.5 * (1.0 + lax.erf(before * 0.7071067811865476))
    hidden = (before * normal_cdf).astype(BF16)
    output = (resid + dot_nn(hidden, fc2_full) + fc2b).astype(BF16)

    def to_tile(field):
        field = field.reshape(-1, ROWS, dim)[:, :CELLS]
        return from_windows(field, batch, tile_rows, tile_cols)

    output = to_tile(output)

    grad_fc2 = dot_tn(hidden, grad_out)
    grad_fc2b = jnp.sum(grad_out.astype(F32), 0)
    grad_hidden = dot_nt(grad_out, fc2_full)
    normal_pdf = jnp.exp(-0.5 * before * before) * 0.3989422804014327
    grad_before = (grad_hidden * (normal_cdf + before * normal_pdf)).astype(BF16)
    grad_fc1 = dot_tn(second, grad_before)
    grad_fc1b = jnp.sum(grad_before.astype(F32), 0)
    grad_second = dot_nt(grad_before, fc1_full)
    grad_gain2 = jnp.sum(grad_second * unit_two, 0)
    grad_shift2 = jnp.sum(grad_second, 0)
    grad_resid = grad_out.astype(F32) + normalize_back(grad_second, unit_two, scaled_two, gain_two)
    grad_pbias = jnp.sum(grad_resid, 0)
    grad_branch = grad_resid.astype(BF16)
    grad_proj = dot_tn(mixed, grad_branch)
    grad_mixed = dot_nt(grad_branch, proj_full).astype(BF16)
    grad_qkv_rows, score_sum = attend_back(qkv, grad_mixed, probs, heads)
    score_sum = score_sum.reshape(heads, PAIR, PAIR)
    score_sum = score_sum[:, :ROWS, :ROWS] + score_sum[:, ROWS:, ROWS:]
    grad_table = jnp.dot(score_sum.reshape(heads, -1), onehot, precision=HIGHEST).T
    grad_qkv = dot_tn(first, grad_qkv_rows)
    grad_qkvb = jnp.sum(grad_qkv_rows.astype(F32), 0)
    grad_first = dot_nt(grad_qkv_rows, qkv_full).astype(BF16).astype(F32)
    grad_gain1 = jnp.sum(grad_first * unit_one, 0)
    grad_shift1 = jnp.sum(grad_first, 0)
    input_grad = normalize_back(grad_first, unit_one, scaled_one, gain_one) + grad_resid
    input_grad = to_tile(input_grad.astype(BF16))

    def rows_of(matrix):
        return [m.reshape(count, share, dim) for m in columns(matrix.astype(BF16))]

    vectors = [
        grad_gain1, grad_shift1, grad_qkvb[:dim], grad_qkvb[2 * dim :], grad_pbias, grad_gain2,
        grad_shift2, grad_fc2b, grad_fc1b,
    ]
    table_row = -(-small_size // dim)
    table_size = -(-grad_table.size // count)
    short = jnp.concatenate([v.reshape(count, -1) for v in vectors], 1)
    short = jnp.pad(short, ((0, 0), (0, table_row * dim - small_size)))
    spread = jnp.pad(grad_table.reshape(-1), (0, table_size * count - grad_table.size))
    short = jnp.concatenate([short, spread.reshape(count, -1)], 1)
    short = jnp.pad(short, ((0, 0), (0, tail * dim - short.shape[1]))).reshape(count, tail, dim)
    grads = jnp.concatenate(
        rows_of(grad_qkv)
        + rows_of(grad_proj)
        + rows_of(grad_fc1)
        + [grad_fc2.astype(BF16).reshape(count, -1, dim), short.astype(BF16)],
        1,
    )
    edges = [edges_behind(output), edges_behind(input_grad)]
    summed, tables, *blocks = reduce_all(grads, pack_edges(edges), low, seq_count, count)
    blocks = unpack_edges(blocks, edges)
    output = join_behind(output, *blocks[0]).reshape(tokens.shape)
    input_grad = join_behind(input_grad, *blocks[1]).reshape(tokens.shape)
    summed = summed.astype(F32)

    def matrix_sum(at, blocks_wide):
        parts = [summed[at + j * share : at + (j + 1) * share] for j in range(blocks_wide)]
        return parts[0] if blocks_wide == 1 else jnp.concatenate(parts, 1)

    sum_qkv = matrix_sum(0, 3)
    sum_proj = matrix_sum(3 * share, 1)
    sum_fc1 = matrix_sum(4 * share, wide)
    sum_fc2 = summed[(4 + wide) * share : low]
    short = summed[low:].reshape(-1)
    owned, at = [], 0
    for v in vectors:
        size = v.shape[0] // count
        owned.append(short[at : at + size])
        at += size
    table_total = tables.astype(F32)[:, table_row:].reshape(count, -1)[:, :table_size]
    table_total = table_total.reshape(-1)[: bias_table.size].reshape(bias_table.shape)
    s_gain1, s_shift1, s_qb, s_vb, s_pb, s_gain2, s_shift2, s_fc2b, s_fc1b = owned
    return (
        output,
        input_grad,
        s_gain1,
        s_shift1,
        sum_qkv,
        s_qb,
        s_vb,
        sum_proj,
        s_pb,
        s_gain2,
        s_shift2,
        sum_fc1,
        s_fc1b,
        sum_fc2,
        s_fc2b,
        table_total,
    )


def solution(mesh):
    rows, vector, matrix, whole = P("dp", "seq", None, None), P("dp"), P("dp", None), P()
    params = (
        vector, vector, matrix, vector, vector, matrix, vector, vector, vector, matrix, vector, matrix, vector,
    )
    in_specs = (rows, rows) + params + (whole, whole, whole)
    out_specs = (rows, rows) + params + (whole,)
    return jax.shard_map(local, mesh=mesh, in_specs=in_specs, out_specs=out_specs, check_vma=False)
```

```python
import functools

import jax
import jax.numpy as jnp
from jax import lax
from jax.experimental import pallas as pl
from jax.experimental.pallas import tpu as pltpu
from jax.sharding import PartitionSpec as P

HIGHEST = lax.Precision.HIGHEST
F32 = jnp.float32
BF16 = jnp.bfloat16
SIDE = 7
CELLS = SIDE * SIDE
ROWS = 56
PAIR = 2 * ROWS
VMEM = 56 * 1024 * 1024


MESH = pl.DeviceIdType.MESH
TILE = 16
STEP = 3


def edges_ahead(field):
    return field[:, :STEP, STEP:], field[:, STEP:, :STEP], field[:, :STEP, :STEP]


def edges_behind(field):
    return field[:, -STEP:, :-STEP], field[:, :-STEP, -STEP:], field[:, -STEP:, -STEP:]


def join_ahead(field, below, beside, corner):
    top = jnp.concatenate([field[:, STEP:, STEP:], beside], 2)
    return jnp.concatenate([top, jnp.concatenate([below, corner], 2)], 1)


def join_behind(field, above, beside, corner):
    low = jnp.concatenate([beside, field[:, :-STEP, :-STEP]], 2)
    return jnp.concatenate([jnp.concatenate([corner, above], 2), low], 1)


def pack_edges(edges):
    packed = []
    for blocks in zip(*edges):
        rows = jnp.concatenate([b.reshape(-1, b.shape[-1]) for b in blocks], 0)
        packed.append(jnp.pad(rows, ((0, -rows.shape[0] % TILE), (0, 0))))
    return packed


def unpack_edges(packed, edges):
    fields = [[] for _ in edges]
    for rows, blocks in zip(packed, zip(*edges)):
        at = 0
        for field, b in zip(fields, blocks):
            size = b.size // b.shape[-1]
            field.append(rows[at : at + size].reshape(b.shape))
            at += size
    return fields


class Mail:
    def __init__(self, send, recv):
        self.send, self.recv, self.used, self.open = send, recv, 0, []

    def push(self, src, dst, seq, dp):
        copy = pltpu.make_async_remote_copy(
            src_ref=src,
            dst_ref=dst,
            send_sem=self.send.at[self.used],
            recv_sem=self.recv.at[self.used],
            device_id=(seq, dp),
            device_id_type=MESH,
        )
        copy.start()
        self.used += 1
        self.open.append(copy)
        return copy

    def close(self):
        for copy in self.open:
            copy.wait_send()


def places(n, nd):
    s, d = lax.axis_index("seq"), lax.axis_index("dp")
    core = d % 2
    row = s + 1 - 2 * (s % 2)
    col = (s + 2) % n
    one = (1 - core) * row + core * col
    two = core * row + (1 - core) * col
    return s, d, one, two, (s // 2 * 2 + 2) % n + 1 - s % 2


def greet(n, nd, s, d):
    barrier = pltpu.get_barrier_semaphore()
    for m in range(1, n):
        pl.semaphore_signal(barrier, inc=1, device_id=((s + m) % n, d), device_id_type=MESH)
    for m in range(1, nd):
        pl.semaphore_signal(barrier, inc=1, device_id=(s, (d + m) % nd), device_id_type=MESH)
    pl.semaphore_wait(barrier, n - 1 + nd - 1)


def edge_sends(mail, n, s, d, src, dst, cols):
    row = s + 1 - 2 * (s % 2)
    col = (s + 2 * cols + n) % n
    return [
        mail.push(src[0], dst[0], row, d),
        mail.push(src[1], dst[1], col, d),
        mail.push(src[2], dst[2], col + 1 - 2 * (col % 2), d),
    ]


def gather_kernel(n, nd, w_ref, e0, e1, e2, o_ref, f0, f1, f2, send, recv, own):
    s, d, one, two, far = places(n, nd)
    nz, core = nd // 2, d % 2
    z = d // 2
    mate = d + 1 - 2 * core
    quarter = w_ref.shape[0] // n

    def part(block, q, span):
        return o_ref.at[block, pl.ds(pl.multiple_of(q * quarter + span[0], TILE), span[1])]

    greet(n, nd, s, d)
    mail = Mail(send, recv)
    keep = pltpu.make_async_copy(w_ref, o_ref.at[d], own)
    keep.start()
    spans = chunks(quarter)
    along = []
    for span in spans:
        mine = w_ref.at[pl.ds(pl.multiple_of(s * quarter + span[0], TILE), span[1])]
        for k in range(1, nz):
            copy = mail.push(mine, part(d, s, span), s, (z + k) % nz * 2 + core)
            along.append((copy, (z + nz - k) % nz * 2 + core, span))
    waits = edge_sends(mail, n, s, d, (e0, e1, e2), (f0, f1, f2), -1)
    waits.append(mail.push(w_ref, o_ref.at[d], s, mate))

    def spread(group):
        across = []
        for copy, block, span in group:
            copy.wait_recv()
            piece = part(block, s, span)
            peers = [(one, one), (two, two)]
            if n != 4:
                peers = [((s + m) % n, (s + n - m) % n) for m in range(1, n)]
            sent = [(mail.push(piece, piece, to, d), source) for to, source in peers]
            across.append((sent, block, span))
            waits.append(mail.push(piece, piece, s, mate))
        return across

    def relay(across):
        for sent, block, span in across:
            for at, (copy, source) in enumerate(sent):
                copy.wait_recv()
                piece = part(block, source, span)
                if n == 4 and at == 0:
                    sent.append((mail.push(piece, piece, two, d), far))
                waits.append(mail.push(piece, piece, s, mate))

    before = []
    for at in range(len(spans)):
        after = spread(along[at * (nz - 1) : (at + 1) * (nz - 1)])
        relay(before)
        before = after
    relay(before)
    for copy in waits:
        copy.wait_recv()
    mail.close()
    keep.wait()


def chunks(rows):
    return [(0, rows)]


def gather_all(shard, edges, n, nd):
    count = len(chunks(shard.shape[0] // n)) * (nd // 2 - 1) * 2 * n + 4
    any_spec = pl.BlockSpec(memory_space=pl.ANY)
    shapes = [jax.ShapeDtypeStruct((nd,) + shard.shape, shard.dtype)]
    shapes += [jax.ShapeDtypeStruct(e.shape, e.dtype) for e in edges]
    return pl.pallas_call(
        functools.partial(gather_kernel, n, nd),
        out_shape=shapes,
        in_specs=[any_spec] * 4,
        out_specs=[any_spec] * 4,
        scratch_shapes=[
            pltpu.SemaphoreType.DMA((count,)),
            pltpu.SemaphoreType.DMA((count,)),
            pltpu.SemaphoreType.DMA,
        ],
        compiler_params=pltpu.CompilerParams(collective_id=0, has_side_effects=True),
    )(shard, *edges)


def reduce_kernel(n, nd, low, g_ref, e0, e1, e2, o_ref, t_ref, f0, f1, f2, held, ra, rb, mid, q_ref, rc, send, recv, own):
    s, d, one, two, far = places(n, nd)
    nz, core = nd // 2, d % 2
    z = d // 2
    mate = d + 1 - 2 * core
    quarter = o_ref.shape[0] // n

    def rows(q):
        return pl.ds(pl.multiple_of(q * quarter, TILE), quarter)

    greet(n, nd, s, d)
    mail = Mail(send, recv)
    order = list(range(1, nz)) + [0]
    first = [
        mail.push(g_ref.at[(z + k) % nz * 2 + 1 - core], ra.at[k], s, mate) for k in order
    ]
    second, third = {}, []

    def across(k, copy):
        copy.wait_recv()
        held[k] = g_ref[(z + k) % nz * 2 + core] + ra[k]
        peers = [(far, one), (one, one)]
        if n != 4:
            peers = [((s + m) % n, (s + m) % n) for m in range(1, n)]
        second[k] = [
            mail.push(held.at[k, rows(q)], rb.at[k, at], to, d) for at, (q, to) in enumerate(peers)
        ]

    def relay(k):
        if n == 4:
            second[k][0].wait_recv()
            mid[k] = held[k, rows(two)] + rb[k, 0]
            second[k].append(mail.push(mid.at[k], rb.at[k, 2], two, d))

    def along(k):
        total = held[k, rows(s)].astype(F32)
        for at in range(1 if n == 4 else 0, n - 1):
            second[k][at].wait_recv()
            total = total + rb[k, at].astype(F32)
        q_ref[k] = total.astype(BF16)
        if k:
            third.append(mail.push(q_ref.at[k], rc.at[k - 1], s, (z + k) % nz * 2 + core))

    for step in range(nz + 2):
        if step < nz:
            across(order[step], first[step])
        if 0 <= step - 1 < nz:
            relay(order[step - 1])
        if 0 <= step - 2:
            along(order[step - 2])
    edge = edge_sends(mail, n, s, d, (e0, e1, e2), (f0, f1, f2), 1)
    total = q_ref[0].astype(F32)
    for k, copy in enumerate(third):
        copy.wait_recv()
        total = total + rc[k].astype(F32)
    o_ref[rows(s)] = total.astype(BF16)
    mine = o_ref.at[rows(s)]
    if n == 4:
        a, b = mail.push(mine, mine, one, d), mail.push(mine, mine, two, d)
        a.wait_recv()
        block = o_ref.at[rows(one)]
        last = [b, mail.push(block, block, two, d)]
    else:
        last = [mail.push(mine, mine, (s + m) % n, d) for m in range(1, n)]
    for copy in last:
        copy.wait_recv()
    table = o_ref.at[pl.ds(low, TILE)]
    keep = pltpu.make_async_copy(table, t_ref.at[d], own)
    keep.start()
    tables = [mail.push(table, t_ref.at[d], s, (d + m) % nd) for m in range(1, nd)]
    for copy in tables + edge:
        copy.wait_recv()
    mail.close()
    keep.wait()


def reduce_all(grads, edges, low, n, nd):
    nz = nd // 2
    rows, width = grads.shape[1:]
    quarter = rows // n
    count = nz * 4 + nz * n + n + nd + 8
    any_spec = pl.BlockSpec(memory_space=pl.ANY)
    vmem_spec = pl.BlockSpec(memory_space=pltpu.VMEM)
    shapes = [
        jax.ShapeDtypeStruct((rows, width), BF16),
        jax.ShapeDtypeStruct((nd, TILE, width), BF16),
    ]
    shapes += [jax.ShapeDtypeStruct(e.shape, e.dtype) for e in edges]
    return pl.pallas_call(
        functools.partial(reduce_kernel, n, nd, low),
        out_shape=shapes,
        in_specs=[vmem_spec] + [any_spec] * 3,
        out_specs=[vmem_spec, vmem_spec] + [any_spec] * 3,
        scratch_shapes=[
            pltpu.VMEM((nz, rows, width), BF16),
            pltpu.VMEM((nz, rows, width), BF16),
            pltpu.VMEM((nz, n - 1, quarter, width), BF16),
            pltpu.VMEM((nz, quarter, width), BF16),
            pltpu.VMEM((nz, quarter, width), BF16),
            pltpu.VMEM((nz - 1 if nz > 1 else 1, quarter, width), BF16),
            pltpu.SemaphoreType.DMA((count,)),
            pltpu.SemaphoreType.DMA((count,)),
            pltpu.SemaphoreType.DMA,
        ],
        compiler_params=pltpu.CompilerParams(
            collective_id=1, has_side_effects=True, vmem_limit_bytes=VMEM
        ),
    )(grads, *edges)


def to_windows(field):
    batch, rows, cols, width = field.shape
    return (
        field.reshape(batch, rows // SIDE, SIDE, cols // SIDE, SIDE, width)
        .transpose(0, 1, 3, 2, 4, 5)
        .reshape(-1, CELLS, width)
    )


def from_windows(blocks, batch, rows, cols):
    width = blocks.shape[-1]
    return (
        blocks.reshape(batch, rows // SIDE, cols // SIDE, SIDE, SIDE, width)
        .transpose(0, 1, 3, 2, 4, 5)
        .reshape(batch, rows, cols, width)
    )


def pad_windows(field):
    return jnp.pad(to_windows(field), ((0, 0), (0, ROWS - CELLS), (0, 0))).reshape(
        -1, field.shape[-1]
    )


def stack_heads(block, per):
    part = lax.broadcasted_iota(jnp.int32, block.shape, 1) // (block.shape[1] // per)
    return jnp.concatenate([jnp.where(part == j, block, jnp.zeros_like(block)) for j in range(per)], 0)


def merge_heads(tall, per):
    rows = tall.shape[0] // per
    part = lax.broadcasted_iota(jnp.int32, (rows, tall.shape[1]), 1) // (tall.shape[1] // per)
    total = jnp.where(part == 0, tall[:rows], 0.0)
    for j in range(1, per):
        total = jnp.where(part == j, tall[j * rows : (j + 1) * rows], total)
    return total


def dot_nt(left, right):
    return lax.dot_general(left, right, (((1,), (1,)), ((), ())), preferred_element_type=F32)


def dot_tn(left, right):
    return lax.dot_general(left, right, (((0,), (0,)), ((), ())), preferred_element_type=F32)


def dot_nn(left, right):
    return jnp.dot(left, right, preferred_element_type=F32)


def attend_kernel(scale, per, qkv_ref, bias_ref, mask_ref, o_ref, p_ref):
    dim = o_ref.shape[1]
    tall = per * PAIR
    mask = mask_ref[0]
    for g in range(dim // 128):
        at = slice(g * 128, (g + 1) * 128)
        band = slice(g * tall, (g + 1) * tall)
        q = stack_heads(qkv_ref[:, g * 128 : (g + 1) * 128], per)
        k = qkv_ref[:, dim + g * 128 : dim + (g + 1) * 128]
        v = qkv_ref[:, 2 * dim + g * 128 : 2 * dim + (g + 1) * 128]
        s = dot_nt(q, k) * scale
        s = s.reshape(per, 2, ROWS, PAIR) + bias_ref[g * per : (g + 1) * per][:, None]
        s = (s.reshape(per, PAIR, PAIR) + mask[None]).reshape(tall, PAIR)
        e = jnp.exp(s - jnp.max(s, -1, keepdims=True))
        p = (e * (1.0 / jnp.sum(e, -1, keepdims=True))).astype(BF16)
        p_ref[0, band, :] = p
        o_ref[:, at] = merge_heads(dot_nn(p, v), per).astype(BF16)


def attend_back_kernel(scale, per, qkv_ref, do_ref, p_ref, dqkv_ref, sum_ref):
    dim = do_ref.shape[1]
    tall = per * PAIR

    @pl.when(pl.program_id(0) == 0)
    def _():
        sum_ref[...] = jnp.zeros_like(sum_ref)

    for g in range(dim // 128):
        band = slice(g * tall, (g + 1) * tall)
        q = stack_heads(qkv_ref[:, g * 128 : (g + 1) * 128], per)
        k = qkv_ref[:, dim + g * 128 : dim + (g + 1) * 128]
        v = qkv_ref[:, 2 * dim + g * 128 : 2 * dim + (g + 1) * 128]
        do = stack_heads(do_ref[:, g * 128 : (g + 1) * 128], per)
        p = p_ref[0, band, :]
        pf = p.astype(F32)
        dp = dot_nt(do, v)
        dl = (pf * (dp - jnp.sum(dp * pf, -1, keepdims=True))).astype(BF16)
        sum_ref[band, :] += dl.astype(F32)
        dq = merge_heads(dot_nn(dl, k), per) * scale
        dk = dot_tn(dl, q) * scale
        dv = dot_tn(p, do)
        dqkv_ref[:, g * 128 : (g + 1) * 128] = dq.astype(BF16)
        dqkv_ref[:, dim + g * 128 : dim + (g + 1) * 128] = dk.astype(BF16)
        dqkv_ref[:, 2 * dim + g * 128 : 2 * dim + (g + 1) * 128] = dv.astype(BF16)


def attend(qkv, bias, mask, heads):
    rows, dim = qkv.shape[0], qkv.shape[1] // 3
    pairs = rows // PAIR
    per = 128 * heads // dim
    return pl.pallas_call(
        functools.partial(attend_kernel, (dim // heads) ** -0.5, per),
        grid=(pairs,),
        out_shape=(
            jax.ShapeDtypeStruct((rows, dim), BF16),
            jax.ShapeDtypeStruct((pairs, heads * PAIR, PAIR), BF16),
        ),
        in_specs=[
            pl.BlockSpec((PAIR, 3 * dim), lambda i: (i, 0)),
            pl.BlockSpec((heads, ROWS, PAIR), lambda i: (0, 0, 0)),
            pl.BlockSpec((1, PAIR, PAIR), lambda i: (i, 0, 0)),
        ],
        out_specs=(
            pl.BlockSpec((PAIR, dim), lambda i: (i, 0)),
            pl.BlockSpec((1, heads * PAIR, PAIR), lambda i: (i, 0, 0)),
        ),
        compiler_params=pltpu.CompilerParams(vmem_limit_bytes=VMEM),
        cost_estimate=pl.CostEstimate(
            flops=4 * rows * heads * PAIR * 128, bytes_accessed=rows * dim * 8, transcendentals=rows * heads * 128
        ),
    )(qkv, bias, mask)


def attend_back(qkv, grad, probs, heads):
    rows, dim = grad.shape
    pairs = rows // PAIR
    per = 128 * heads // dim
    return pl.pallas_call(
        functools.partial(attend_back_kernel, (dim // heads) ** -0.5, per),
        grid=(pairs,),
        out_shape=(
            jax.ShapeDtypeStruct((rows, 3 * dim), BF16),
            jax.ShapeDtypeStruct((heads * PAIR, PAIR), F32),
        ),
        in_specs=[
            pl.BlockSpec((PAIR, 3 * dim), lambda i: (i, 0)),
            pl.BlockSpec((PAIR, dim), lambda i: (i, 0)),
            pl.BlockSpec((1, heads * PAIR, PAIR), lambda i: (i, 0, 0)),
        ],
        out_specs=(
            pl.BlockSpec((PAIR, 3 * dim), lambda i: (i, 0)),
            pl.BlockSpec((heads * PAIR, PAIR), lambda i: (0, 0)),
        ),
        compiler_params=pltpu.CompilerParams(vmem_limit_bytes=VMEM),
        cost_estimate=pl.CostEstimate(
            flops=8 * rows * heads * PAIR * 128, bytes_accessed=rows * dim * 16, transcendentals=0
        ),
    )(qkv, grad, probs)


def normalize(values):
    center = values - jnp.mean(values, -1, keepdims=True)
    scaled = lax.rsqrt(jnp.mean(center * center, -1, keepdims=True) + 1e-05)
    return center * scaled, scaled


def normalize_back(grad, unit, scaled, gain):
    inner = grad * gain
    return scaled * (
        inner
        - jnp.mean(inner, -1, keepdims=True)
        - unit * jnp.mean(inner * unit, -1, keepdims=True)
    )


def local(
    tokens,
    cotangent,
    norm1_gain,
    norm1_bias,
    qkv_weight,
    query_bias,
    value_bias,
    proj_weight,
    proj_bias,
    norm2_gain,
    norm2_bias,
    fc1_weight,
    fc1_bias,
    fc2_weight,
    fc2_bias,
    bias_table,
    region_ids,
    rel_index,
):
    batch = tokens.shape[0]
    dim = tokens.shape[-1]
    heads = bias_table.shape[1]
    image_rows, image_cols = region_ids.shape
    seq_count = lax.axis_size("seq")
    tile_rows = image_rows // 2
    tile_cols = image_cols * 2 // seq_count
    place = lax.axis_index("seq")

    count = lax.axis_size("dp")
    share = dim // count
    wide = fc1_weight.shape[1] // dim

    smalls = [
        norm1_gain, norm1_bias, query_bias, value_bias, proj_bias, norm2_gain, norm2_bias, fc2_bias, fc1_bias,
    ]
    low = share * (4 + 2 * wide)
    total_rows = -(-(low + TILE) // (TILE * seq_count)) * TILE * seq_count
    tail = total_rows - low
    short = jnp.concatenate(smalls)
    small_size = short.shape[0]
    short = jnp.pad(short, (0, tail * dim - small_size)).reshape(tail, dim)

    def columns(matrix):
        return [matrix[:, at : at + dim] for at in range(0, matrix.shape[1], dim)]

    shard = jnp.concatenate(
        columns(qkv_weight) + [proj_weight] + columns(fc1_weight) + [fc2_weight, short], 0
    )
    tile = tokens.reshape(batch, tile_rows, tile_cols, dim)
    grad_tile = cotangent.reshape(batch, tile_rows, tile_cols, dim)
    edges = [edges_ahead(tile), edges_ahead(grad_tile)]
    gathered, *blocks = gather_all(shard, pack_edges(edges), seq_count, count)
    blocks = unpack_edges(blocks, edges)

    def matrix_of(at, blocks_wide):
        parts = [
            gathered[:, at + j * share : at + (j + 1) * share].reshape(dim, dim) for j in range(blocks_wide)
        ]
        return parts[0] if blocks_wide == 1 else jnp.concatenate(parts, 1)

    qkv_full = matrix_of(0, 3)
    proj_full = matrix_of(3 * share, 1)
    fc1_full = matrix_of(4 * share, wide)
    fc2_full = gathered[:, (4 + wide) * share : low].reshape(-1, dim)
    small_all = gathered[:, low:].reshape(count, -1)
    full, at = [], 0
    for v in smalls:
        full.append(small_all[:, at : at + v.shape[0]].reshape(-1).astype(F32))
        at += v.shape[0]
    gain_one, shift_one, qbias, vbias, pbias, gain_two, shift_two, fc2b, fc1b = full

    regions = lax.dynamic_slice(
        region_ids, (place % 2 * tile_rows, place // 2 * tile_cols), (tile_rows, tile_cols)
    )
    region_win = to_windows(regions[None, :, :, None])[:, :, 0]
    region_win = jnp.pad(region_win, ((0, 0), (0, ROWS - CELLS)), constant_values=-1)
    region_win = jnp.tile(region_win.reshape(-1, PAIR), (batch, 1))
    half = jnp.arange(PAIR, dtype=jnp.int32) // ROWS
    mask = jnp.where(region_win[:, :, None] == region_win[:, None, :], 0.0, -100.0).astype(F32)
    shut = (half[:, None] != half[None, :])[None] | (region_win < 0)[:, None, :]
    mask = jnp.where(shut, -1e30, mask)
    index = jnp.pad(rel_index, ((0, ROWS - CELLS), (0, ROWS - CELLS)))
    names = jnp.arange(bias_table.shape[0], dtype=jnp.int32)
    onehot = (index.reshape(-1)[:, None] == names[None, :]).astype(F32)
    twice = jnp.tile(index, (1, 2)).reshape(-1)
    bias = jnp.dot(
        bias_table.T, (names[:, None] == twice[None, :]).astype(F32), precision=HIGHEST
    ).reshape(heads, ROWS, PAIR)

    source = pad_windows(join_ahead(tile, *blocks[0]))
    grad_out = pad_windows(join_ahead(grad_tile, *blocks[1]))
    source = source.astype(F32)

    unit_one, scaled_one = normalize(source)
    first = (unit_one * gain_one + shift_one).astype(BF16)
    qkv_bias = jnp.concatenate([qbias, jnp.zeros((dim,), F32), vbias])
    qkv = (dot_nn(first, qkv_full) + qkv_bias).astype(BF16)
    mixed, probs = attend(qkv, bias, mask, heads)
    resid = source + dot_nn(mixed, proj_full) + pbias
    unit_two, scaled_two = normalize(resid)
    second = (unit_two * gain_two + shift_two).astype(BF16)
    before = dot_nn(second, fc1_full) + fc1b
    normal_cdf = 0.5 * (1.0 + lax.erf(before * 0.7071067811865476))
    hidden = (before * normal_cdf).astype(BF16)
    output = (resid + dot_nn(hidden, fc2_full) + fc2b).astype(BF16)

    def to_tile(field):
        field = field.reshape(-1, ROWS, dim)[:, :CELLS]
        return from_windows(field, batch, tile_rows, tile_cols)

    output = to_tile(output)

    grad_fc2 = dot_tn(hidden, grad_out)
    grad_fc2b = jnp.sum(grad_out.astype(F32), 0)
    grad_hidden = dot_nt(grad_out, fc2_full)
    normal_pdf = jnp.exp(-0.5 * before * before) * 0.3989422804014327
    grad_before = (grad_hidden * (normal_cdf + before * normal_pdf)).astype(BF16)
    grad_fc1 = dot_tn(second, grad_before)
    grad_fc1b = jnp.sum(grad_before.astype(F32), 0)
    grad_second = dot_nt(grad_before, fc1_full)
    grad_gain2 = jnp.sum(grad_second * unit_two, 0)
    grad_shift2 = jnp.sum(grad_second, 0)
    grad_resid = grad_out.astype(F32) + normalize_back(grad_second, unit_two, scaled_two, gain_two)
    grad_pbias = jnp.sum(grad_resid, 0)
    grad_branch = grad_resid.astype(BF16)
    grad_proj = dot_tn(mixed, grad_branch)
    grad_mixed = dot_nt(grad_branch, proj_full).astype(BF16)
    grad_qkv_rows, score_sum = attend_back(qkv, grad_mixed, probs, heads)
    score_sum = score_sum.reshape(heads, PAIR, PAIR)
    score_sum = score_sum[:, :ROWS, :ROWS] + score_sum[:, ROWS:, ROWS:]
    grad_table = jnp.dot(score_sum.reshape(heads, -1), onehot, precision=HIGHEST).T
    grad_qkv = dot_tn(first, grad_qkv_rows)
    grad_qkvb = jnp.sum(grad_qkv_rows.astype(F32), 0)
    grad_first = dot_nt(grad_qkv_rows, qkv_full).astype(BF16).astype(F32)
    grad_gain1 = jnp.sum(grad_first * unit_one, 0)
    grad_shift1 = jnp.sum(grad_first, 0)
    input_grad = normalize_back(grad_first, unit_one, scaled_one, gain_one) + grad_resid
    input_grad = to_tile(input_grad.astype(BF16))

    def rows_of(matrix):
        return [m.reshape(count, share, dim) for m in columns(matrix.astype(BF16))]

    vectors = [
        grad_gain1, grad_shift1, grad_qkvb[:dim], grad_qkvb[2 * dim :], grad_pbias, grad_gain2,
        grad_shift2, grad_fc2b, grad_fc1b,
    ]
    table_row = -(-small_size // dim)
    table_size = -(-grad_table.size // count)
    short = jnp.concatenate([v.reshape(count, -1) for v in vectors], 1)
    short = jnp.pad(short, ((0, 0), (0, table_row * dim - small_size)))
    spread = jnp.pad(grad_table.reshape(-1), (0, table_size * count - grad_table.size))
    short = jnp.concatenate([short, spread.reshape(count, -1)], 1)
    short = jnp.pad(short, ((0, 0), (0, tail * dim - short.shape[1]))).reshape(count, tail, dim)
    grads = jnp.concatenate(
        rows_of(grad_qkv)
        + rows_of(grad_proj)
        + rows_of(grad_fc1)
        + [grad_fc2.astype(BF16).reshape(count, -1, dim), short.astype(BF16)],
        1,
    )
    edges = [edges_behind(output), edges_behind(input_grad)]
    summed, tables, *blocks = reduce_all(grads, pack_edges(edges), low, seq_count, count)
    blocks = unpack_edges(blocks, edges)
    output = join_behind(output, *blocks[0]).reshape(tokens.shape)
    input_grad = join_behind(input_grad, *blocks[1]).reshape(tokens.shape)
    summed = summed.astype(F32)

    def matrix_sum(at, blocks_wide):
        parts = [summed[at + j * share : at + (j + 1) * share] for j in range(blocks_wide)]
        return parts[0] if blocks_wide == 1 else jnp.concatenate(parts, 1)

    sum_qkv = matrix_sum(0, 3)
    sum_proj = matrix_sum(3 * share, 1)
    sum_fc1 = matrix_sum(4 * share, wide)
    sum_fc2 = summed[(4 + wide) * share : low]
    short = summed[low:].reshape(-1)
    owned, at = [], 0
    for v in vectors:
        size = v.shape[0] // count
        owned.append(short[at : at + size])
        at += size
    table_total = tables.astype(F32)[:, table_row:].reshape(count, -1)[:, :table_size]
    table_total = table_total.reshape(-1)[: bias_table.size].reshape(bias_table.shape)
    s_gain1, s_shift1, s_qb, s_vb, s_pb, s_gain2, s_shift2, s_fc2b, s_fc1b = owned
    return (
        output,
        input_grad,
        s_gain1,
        s_shift1,
        sum_qkv,
        s_qb,
        s_vb,
        sum_proj,
        s_pb,
        s_gain2,
        s_shift2,
        sum_fc1,
        s_fc1b,
        sum_fc2,
        s_fc2b,
        table_total,
    )


def solution(mesh):
    rows, vector, matrix, whole = P("dp", "seq", None, None), P("dp"), P("dp", None), P()
    params = (
        vector, vector, matrix, vector, vector, matrix, vector, vector, vector, matrix, vector, matrix, vector,
    )
    in_specs = (rows, rows) + params + (whole, whole, whole)
    out_specs = (rows, rows) + params + (whole,)
    return jax.shard_map(local, mesh=mesh, in_specs=in_specs, out_specs=out_specs, check_vma=False)
```
